32 devices in a mesh: var: 4 (over y, core), samp: 8 (over z, x).
Axes of the slice: x: 2, y: 2, z: 4, core: 2. Of those that a mesh axis runs over, the one named last changes fastest.
Arguments:
- dosages: float32 [6144, 4096], P('samp', 'var'), may hold values from 0 to 2
Outputs:
- ld_band: float32 [4096, 1024], P(('var', 'samp'))
The draws below stay inside these ranges and needn't reach their ends.
All inputs are finite; a program needn't handle non-finite values.
Results may differ from the reference program's by a relative error of at most 0.0003.
Values sent between devices are 32-bit elements; how exact they have to be, the bound alone decides.
No kernel may reach another device: no remote copies, remote signals or barrier semaphores. Data moves between devices by JAX's collectives and lax.ppermute only.
A program may use at most 64 MiB of HBM per device.

```python
import jax
import jax.numpy as jnp
from jax import lax

BAND = 1024
VARIANTS = 4096
SAMPLES = 6144


def blend(key, width):
    places = jnp.arange(VARIANTS)
    index = places // width
    frac = (places % width).astype(jnp.float32) / width
    factor = jax.random.normal(key, (SAMPLES, VARIANTS // width + 1), jnp.float32)
    return factor[:, index] * (1.0 - frac) + factor[:, index + 1] * frac


def draw_dosages(key, part):
    key = jax.random.fold_in(key, 11)
    keys = jax.random.split(key, 7)
    loads = jax.random.uniform(keys[3], (3, VARIANTS), jnp.float32, -1.0, 1.0)
    latent = loads[0] * blend(keys[0], BAND // 8)
    latent = latent + loads[1] * blend(keys[1], BAND)
    latent = latent + loads[2] * blend(keys[2], 4 * BAND)
    noise = jax.random.normal(keys[4], (SAMPLES, VARIANTS), jnp.float32)
    spread = jax.random.uniform(keys[5], (VARIANTS,), jnp.float32, 0.6, 1.4)
    offset = jax.random.uniform(keys[6], (VARIANTS,), jnp.float32, -2.0, 2.0)
    latent = latent + 0.7 * noise
    return 2.0 * jax.nn.sigmoid(0.8 * spread * latent + offset)


def setup_inputs(seed: int = 0) -> dict:
    splits = jax.random.split(jax.random.key(seed), 2)
    return {
        "dosages": draw_dosages(jax.random.fold_in(splits[1], 71), 0),
    }


EPS = 1e-06

def band_rows(block, offset):
    rows = block.shape[0]
    cols = block.shape[1]
    width = cols // 2
    flat = jnp.concatenate([block.reshape(-1), jnp.zeros((width + 1,), block.dtype)])
    taken = lax.dynamic_slice_in_dim(flat, offset + 1, rows * (cols + 1))
    return taken.reshape(rows, cols + 1)[:, :width]

def reference(dosages):
    mean = lax.optimization_barrier(jnp.sum(dosages, 0)) / SAMPLES
    centered = dosages - mean
    spread = lax.optimization_barrier(jnp.sum(centered * centered, 0)) / SAMPLES
    scale = lax.rsqrt(spread + EPS)
    padded = jnp.concatenate([centered, jnp.zeros((SAMPLES, BAND), jnp.float32)], 1)
    scale_pad = jnp.concatenate([scale, jnp.zeros((BAND,), jnp.float32)])

    def one_block(index):
        start = (index * BAND).astype(jnp.int32)
        own = lax.dynamic_slice_in_dim(centered, start, BAND, 1)
        wide = lax.dynamic_slice_in_dim(padded, start, 2 * BAND, 1)
        gram = lax.dot_general(own, wide, (((0,), (0,)), ((), ())), precision=lax.Precision.HIGHEST, preferred_element_type=jnp.float32)
        wide_scale = lax.dynamic_slice_in_dim(scale_pad, start, 2 * BAND)
        own_scale = lax.dynamic_slice_in_dim(scale, start, BAND)
        return band_rows(gram * wide_scale[None, :], 0) * own_scale[:, None] / SAMPLES
    blocks = lax.map(one_block, jnp.arange(VARIANTS // BAND, dtype=jnp.int32))
    return blocks.reshape(VARIANTS, BAND)
```

```python
import functools

import jax
import jax.numpy as jnp
from jax import lax
from jax.experimental import pallas as pl
from jax.experimental.pallas import tpu as pltpu
from jax.sharding import PartitionSpec as P

EPS = 1e-06
STATS = 8
VMEM = pl.BlockSpec(memory_space=pltpu.VMEM)


def params(mib):
    return pltpu.CompilerParams(vmem_limit_bytes=mib << 20)


def cost(flops, data):
    return pl.CostEstimate(flops=flops, bytes_accessed=data, transcendentals=0)


def split(value):
    high = value.astype(jnp.bfloat16)
    low = (value - high.astype(jnp.float32)).astype(jnp.bfloat16)
    return high, low


def centre(block):
    count = block.shape[0]
    mean = jnp.sum(block, 0, keepdims=True) / count
    centred = block - mean
    left = jnp.sum(centred, 0, keepdims=True) / count
    squares = jnp.sum(centred * centred, 0, keepdims=True)
    return centred, mean, left, squares


def prepare_kernel(block, high, low, high_t, low_t, stats):
    centred, mean, left, squares = centre(block[...])
    high[...], low[...] = split(centred)
    high_t[...], low_t[...] = split(centred.T)
    zero = jnp.zeros_like(mean)
    rows = [mean, zero, left, zero, squares, zero, zero, zero]
    stats[...] = jnp.concatenate(rows, 0)


def prepare(dosages, width):
    samples, cols = dosages.shape
    tall = pl.BlockSpec((samples, width), lambda i: (0, i))
    flat = pl.BlockSpec((width, samples), lambda i: (i, 0))
    half = jax.ShapeDtypeStruct((samples, cols), jnp.bfloat16)
    half_t = jax.ShapeDtypeStruct((cols, samples), jnp.bfloat16)
    return pl.pallas_call(
        prepare_kernel,
        grid=(cols // width,),
        in_specs=[tall],
        out_specs=[tall, tall, flat, flat, pl.BlockSpec((STATS, width), lambda i: (0, i))],
        out_shape=[half, half, half_t, half_t, jax.ShapeDtypeStruct((STATS, cols), jnp.float32)],
        compiler_params=params(32),
        cost_estimate=cost(10 * samples * cols, 12 * samples * cols),
        name="prepare",
    )(dosages)


def place(owner, me, order):
    apart = jnp.bitwise_xor(owner, me)
    spot = 0
    for bit in order:
        spot = spot * 2 + (lax.shift_right_logical(apart, bit) & 1)
    return spot


def product(high_t, low_t, rows, high, low):
    dot = functools.partial(jnp.dot, preferred_element_type=jnp.float32)
    a, b = high_t[rows, :], low_t[rows, :]
    return dot(a, high) + (dot(a, low) + dot(b, high))


def gram_kernel(parts, start, order, high_t, low_t, high, low, own_stats, ahead, send, keep):
    cols = high_t.shape[0]
    width = ahead.shape[1]
    share = cols // parts
    half = parts // 2
    me = lax.axis_index("samp")
    centred, mean, left, squares = centre(ahead[...])
    ahead_high, ahead_low = split(centred)
    own_high, own_low = high[...], low[...]
    mine = own_stats[...]
    rows = [mine[0:1], mean, mine[2:3], left, mine[4:5], squares, mine[6:8]]
    stats = jnp.concatenate(rows, 0)
    send[half * share :, :] = stats
    keep[half * share :, :] = stats
    for first in range(0, cols, width):
        band = pl.ds(first, width)
        if first <= start:
            tile = product(high_t, low_t, band, own_high, own_low)
        if first >= start:
            later = product(high_t, low_t, band, ahead_high, ahead_low)
        if first > start:
            tile = later
        if first == start:
            row = lax.broadcasted_iota(jnp.int32, tile.shape, 0)
            col = lax.broadcasted_iota(jnp.int32, tile.shape, 1)
            tile = jnp.where(col > row, tile, later)
        for part in range(width // share):
            spot = place(first // share + part, me, order)
            piece = tile[part * share : (part + 1) * share]
            there = pl.ds(pl.multiple_of((spot & (half - 1)) * share, share), share)

            @pl.when(spot >= half)
            def _():
                send[there, :] = piece

            @pl.when(spot < half)
            def _():
                keep[there, :] = piece


def gram(parts, start, order, high_t, low_t, high, low, stats, ahead):
    cols, samples = high_t.shape
    width = ahead.shape[1]
    index = start // width
    tall = pl.BlockSpec((samples, width), lambda i: (0, index))
    whole = pl.BlockSpec((cols, samples), lambda i: (0, 0))
    shape = (cols // 2 + STATS, width)
    out = jax.ShapeDtypeStruct(shape, jnp.float32)
    return pl.pallas_call(
        functools.partial(gram_kernel, parts, start, order),
        grid=(1,),
        in_specs=[
            whole,
            whole,
            tall,
            tall,
            pl.BlockSpec((STATS, width), lambda i: (0, index)),
            pl.BlockSpec((samples, width), lambda i: (0, 0)),
        ],
        out_specs=[pl.BlockSpec(shape, lambda i: (0, 0))] * 2,
        out_shape=[out, out],
        compiler_params=params(40),
        cost_estimate=cost(6 * cols * width * samples, 4 * samples * (cols + 2 * width)),
        name="gram",
    )(high_t, low_t, high, low, stats, ahead)


def halve_kernel(size, keep, got, send, rest):
    half = size // 2
    send[:half, :] = keep[half:size, :] + got[half:size, :]
    rest[:half, :] = keep[:half, :] + got[:half, :]
    stats = keep.shape[0] - size
    for out in (send, rest):
        out[half : half + stats, :] = keep[size:, :]
        out[half + stats :, :] = got[size:, :]


def halve(size, keep, got):
    stats = keep.shape[0] - size
    shape = (size // 2 + 2 * stats, keep.shape[1])
    out = jax.ShapeDtypeStruct(shape, jnp.float32)
    return pl.pallas_call(
        functools.partial(halve_kernel, size),
        in_specs=[VMEM, VMEM],
        out_specs=[VMEM, VMEM],
        out_shape=[out, out],
        compiler_params=params(16),
        cost_estimate=cost(size * keep.shape[1], 16 * size * keep.shape[1]),
        name="halve",
    )(keep, got)


def finish_kernel(parts, samples, pieces, *refs):
    out, body, marks, scales = refs[2 * pieces :]
    share, cols = out.shape
    total = samples * parts
    me = lax.axis_index("samp")
    start = 0
    for i in range(pieces):
        keep, got = refs[2 * i], refs[2 * i + 1]
        width = keep.shape[1]
        here = slice(start, start + width)
        body[:, here] = keep[:share, :] + got[:share, :]
        half = parts // 2
        stats = jnp.concatenate(
            [ref[share:, :].reshape(half, STATS, width) for ref in (keep, got)], 0
        )
        mean = jnp.sum(stats, 0, keepdims=True) / parts
        apart = (stats - mean) + pltpu.roll(stats, STATS - 2, 1)
        apart = apart - jnp.sum(apart, 0, keepdims=True) / parts
        kind = lax.broadcasted_iota(jnp.int32, stats.shape, 1)
        mark = jnp.where(kind < 2, apart, jnp.where(kind < 4, stats, 0.0))
        moved = jnp.sum(mark * mark, 0) * samples
        squares = jnp.sum(stats, 0)
        spread = (squares[4:6] + (moved[0:2] - moved[2:4])) / total
        marks[:, here] = mark.reshape(parts * STATS, width)
        scales[0:2, here] = lax.rsqrt(spread + EPS)
        start += width
    first = me * share
    if share % 128 == 0:
        window = pl.ds(pl.multiple_of(first, 128), share)
        row_marks, row_scale = marks[:, window], scales[0:1, window]
    else:
        inside = lax.rem(first, 128)
        window = pl.ds(pl.multiple_of(first - inside, 128), 128)
        back = lax.rem(128 - inside, 128)
        row_marks = pltpu.roll(marks[:, window], back, 1)[:, :share]
        row_scale = pltpu.roll(jnp.broadcast_to(scales[0:1, window], (8, 128)), back, 1)[0:1, :share]
    row_scale = jnp.broadcast_to(row_scale, (128, share)).T / total
    kind = lax.broadcasted_iota(jnp.int32, row_marks.shape, 0) % STATS
    signed = jnp.where(kind == 0, row_marks, jnp.where(kind == 2, -row_marks, 0.0)) * samples
    signed_next = pltpu.roll(signed, 1, 0)
    dot = functools.partial(
        lax.dot_general,
        dimension_numbers=(((0,), (0,)), ((), ())),
        precision=lax.Precision.HIGHEST,
        preferred_element_type=jnp.float32,
    )
    row = first + lax.broadcasted_iota(jnp.int32, (share, 128), 0)
    lane = lax.broadcasted_iota(jnp.int32, (share, 128), 1)
    own_fix, ahead_fix = dot(signed, marks[...]), dot(signed_next, marks[...])
    for left in range(0, cols, 128):
        here = slice(left, left + 128)
        own = lane + left > row
        fix = jnp.where(own, own_fix[:, here], ahead_fix[:, here])
        scale = jnp.where(own, scales[0:1, here], scales[1:2, here])
        body[:, here] = (body[:, here] + fix) * scale * row_scale
    turned = pltpu.roll(body[...], lax.rem(2 * cols - first - 1, cols), 1)
    row = lax.broadcasted_iota(jnp.int32, (share, cols), 0)
    step = 1
    while step < share:
        moved = pltpu.roll(turned, cols - step, 1)
        turned = jnp.where((row & step) != 0, moved, turned)
        step *= 2
    out[...] = turned


def finish(parts, samples, share, cols, pairs):
    flat = [array for pair in pairs for array in pair]
    return pl.pallas_call(
        functools.partial(finish_kernel, parts, samples, len(pairs)),
        in_specs=[VMEM] * len(flat),
        out_specs=VMEM,
        out_shape=jax.ShapeDtypeStruct((share, cols), jnp.float32),
        scratch_shapes=[
            pltpu.VMEM((share, cols), jnp.float32),
            pltpu.VMEM((parts * STATS, cols), jnp.float32),
            pltpu.VMEM((8, cols), jnp.float32),
        ],
        compiler_params=params(32),
        cost_estimate=cost(40 * share * cols, 16 * share * cols),
        name="finish",
    )(*flat)


def swap(array, bit, parts):
    return lax.ppermute(array, "samp", [(i, i ^ (1 << bit)) for i in range(parts)])


def local(dosages):
    samples, cols = dosages.shape
    parts = lax.axis_size("samp")
    blocks = lax.axis_size("var")
    share = cols // parts
    steps = parts.bit_length() - 1
    unit = cols // 8
    widths = [unit, unit, 2 * unit, 2 * unit, 2 * unit]
    starts = [sum(widths[:i]) for i in range(len(widths))]
    route = [(i, i - 1) for i in range(1, blocks)]
    order = tuple(range(steps))
    ahead = [
        lax.ppermute(dosages[:, start : start + width], "var", route)
        for start, width in zip(starts, widths)
    ]
    high, low, high_t, low_t, stats = prepare(dosages, 2 * unit)
    pairs = []
    for start, block in zip(starts, ahead):
        send, keep = gram(parts, start, order, high_t, low_t, high, low, stats, block)
        size = cols // 2
        for step in order[:-1]:
            got = swap(send, step, parts)
            send, keep = halve(size, keep, got)
            size //= 2
        pairs.append((keep, swap(send, order[-1], parts)))
    return finish(parts, samples, share, cols, pairs)


def solution(mesh):
    in_specs = (P("samp", "var"),)
    out_specs = P(("var", "samp"), None)
    return jax.shard_map(local, mesh=mesh, in_specs=in_specs, out_specs=out_specs, check_vma=False)
```

```python
import functools

import jax
import jax.numpy as jnp
from jax import lax
from jax.experimental import pallas as pl
from jax.experimental.pallas import tpu as pltpu
from jax.sharding import PartitionSpec as P

EPS = 1e-06
STATS = 8
VMEM = pl.BlockSpec(memory_space=pltpu.VMEM)
ANY = pl.BlockSpec(memory_space=pl.ANY)


def params(mib):
    return pltpu.CompilerParams(vmem_limit_bytes=mib << 20)


def cost(flops, data):
    return pl.CostEstimate(flops=flops, bytes_accessed=data, transcendentals=0)


def split(value):
    high = value.astype(jnp.bfloat16)
    low = (value - high.astype(jnp.float32)).astype(jnp.bfloat16)
    return high, low


def centre(block):
    count = block.shape[0]
    mean = jnp.sum(block, 0, keepdims=True) / count
    centred = block - mean
    left = jnp.sum(centred, 0, keepdims=True) / count
    squares = jnp.sum(centred * centred, 0, keepdims=True)
    return centred, mean, left, squares


def prepare_kernel(block, high, low, high_t, low_t, stats):
    centred, mean, left, squares = centre(block[...])
    high[...], low[...] = split(centred)
    high_t[...], low_t[...] = split(centred.T)
    zero = jnp.zeros_like(mean)
    rows = [mean, zero, left, zero, squares, zero, zero, zero]
    stats[...] = jnp.concatenate(rows, 0)


def prepare(dosages, width):
    samples, cols = dosages.shape
    tall = pl.BlockSpec((samples, width), lambda i: (0, i))
    flat = pl.BlockSpec((width, samples), lambda i: (i, 0))
    half = jax.ShapeDtypeStruct((samples, cols), jnp.bfloat16)
    half_t = jax.ShapeDtypeStruct((cols, samples), jnp.bfloat16)
    return pl.pallas_call(
        prepare_kernel,
        grid=(cols // width,),
        in_specs=[tall],
        out_specs=[tall, tall, flat, flat, pl.BlockSpec((STATS, width), lambda i: (0, i))],
        out_shape=[half, half, half_t, half_t, jax.ShapeDtypeStruct((STATS, cols), jnp.float32)],
        compiler_params=params(32),
        cost_estimate=cost(10 * samples * cols, 12 * samples * cols),
        name="prepare",
    )(dosages)


def place(owner, me, order):
    apart = jnp.bitwise_xor(owner, me)
    spot = 0
    for bit in order:
        spot = spot * 2 + (lax.shift_right_logical(apart, bit) & 1)
    return spot


def product(high_t, low_t, rows, high, low):
    dot = functools.partial(jnp.dot, preferred_element_type=jnp.float32)
    a, b = high_t[rows, :], low_t[rows, :]
    return dot(a, high) + (dot(a, low) + dot(b, high))


def gram_kernel(piece, spots, order, high_t, low_t, high, low, own_stats, *refs):
    first, last, start, width = piece
    send, keep = refs[-2:]
    cols = high_t.shape[0]
    share = (last - first) // spots
    half = spots // 2
    me = lax.axis_index("samp")
    own_high, own_low = high[...], low[...]
    mine = own_stats[...]
    if last > start:
        centred, mean, left, squares = centre(refs[0][...])
        ahead_high, ahead_low = split(centred)
        rows = [mine[0:1], mean, mine[2:3], left, mine[4:5], squares, mine[6:8]]
        mine = jnp.concatenate(rows, 0)
    send[half * share :, :] = mine
    keep[half * share :, :] = mine
    tall = min(width, 2 * cols // 8)
    for top in range(first, last, tall):
        band = pl.ds(top, tall)
        if top < start + width:
            tile = product(high_t, low_t, band, own_high, own_low)
        if top + tall > start:
            later = product(high_t, low_t, band, ahead_high, ahead_low)
            if top >= start + width:
                tile = later
            else:
                row = lax.broadcasted_iota(jnp.int32, tile.shape, 0) + top
                col = lax.broadcasted_iota(jnp.int32, tile.shape, 1) + start
                tile = jnp.where(col > row, tile, later)
        for part in range(tall // share):
            spot = place(top // share + part, me, order)
            block = tile[part * share : (part + 1) * share]
            there = pl.ds(pl.multiple_of((spot & (half - 1)) * share, share), share)

            @pl.when(spot >= half)
            def _():
                send[there, :] = block

            @pl.when(spot < half)
            def _():
                keep[there, :] = block


def gram(piece, spots, order, prepared, ahead, after):
    high, low, high_t, low_t, stats = prepared
    first, last, start, width = piece
    cols, samples = high_t.shape
    index = start // width
    tall = pl.BlockSpec((samples, width), lambda i: (0, index))
    whole = pl.BlockSpec((cols, samples), lambda i: (0, 0))
    shape = ((last - first) // 2 + STATS, width)
    out = jax.ShapeDtypeStruct(shape, jnp.float32)
    extra = [] if ahead is None else [ahead]
    return pl.pallas_call(
        functools.partial(gram_kernel, piece, spots, order),
        grid=(1,),
        in_specs=[whole, whole, tall, tall, pl.BlockSpec((STATS, width), lambda i: (0, index))]
        + [pl.BlockSpec((samples, width), lambda i: (0, 0))] * len(extra)
        + [ANY] * len(after),
        out_specs=[pl.BlockSpec(shape, lambda i: (0, 0))] * 2,
        out_shape=[out, out],
        compiler_params=params(40),
        cost_estimate=cost(6 * (last - first) * width * samples, 4 * samples * (cols + 2 * width)),
        name="gram",
    )(high_t, low_t, high, low, stats, *extra, *after)


def cut_kernel(width, count, source, *refs):
    outs, done = refs[-1 - count : -1], refs[-1]
    copies = []
    for i, out in enumerate(outs):
        taken = source.at[:, pl.ds((i + 1) * width, width)]
        copies.append(pltpu.make_async_copy(taken, out, done.at[i]))
    for copy in copies:
        copy.start()
    for copy in copies:
        copy.wait()


def cut(dosages, width, after):
    samples, cols = dosages.shape
    count = cols // width - 1
    block = jax.ShapeDtypeStruct((samples, width), dosages.dtype)
    return pl.pallas_call(
        functools.partial(cut_kernel, width, count),
        in_specs=[ANY] * (1 + len(after)),
        out_specs=[ANY] * count,
        out_shape=[block] * count,
        scratch_shapes=[pltpu.SemaphoreType.DMA((count,))],
        cost_estimate=cost(0, 8 * samples * cols),
        name="cut",
    )(dosages, *after)


def halve_kernel(size, keep, got, *refs):
    send, rest = refs[-2:]
    half = size // 2
    send[:half, :] = keep[half:size, :] + got[half:size, :]
    rest[:half, :] = keep[:half, :] + got[:half, :]
    stats = keep.shape[0] - size
    for out in (send, rest):
        out[half : half + stats, :] = keep[size:, :]
        out[half + stats :, :] = got[size:, :]


def merge_kernel(size, keep, got, *refs):
    out = refs[-1]
    out[:size, :] = keep[:size, :] + got[:size, :]
    stats = keep.shape[0] - size
    out[size : size + stats, :] = keep[size:, :]
    out[size + stats :, :] = got[size:, :]


def halve(size, pair, after):
    keep, got = pair
    stats = keep.shape[0] - size
    shape = (size // 2 + 2 * stats, keep.shape[1])
    out = jax.ShapeDtypeStruct(shape, jnp.float32)
    return pl.pallas_call(
        functools.partial(halve_kernel, size),
        in_specs=[VMEM, VMEM] + [ANY] * len(after),
        out_specs=[VMEM, VMEM],
        out_shape=[out, out],
        compiler_params=params(16),
        cost_estimate=cost(size * keep.shape[1], 16 * size * keep.shape[1]),
        name="halve",
    )(keep, got, *after)


def merge(size, pair, after):
    keep, got = pair
    stats = keep.shape[0] - size
    shape = (size + 2 * stats, keep.shape[1])
    return pl.pallas_call(
        functools.partial(merge_kernel, size),
        in_specs=[VMEM, VMEM] + [ANY] * len(after),
        out_specs=VMEM,
        out_shape=jax.ShapeDtypeStruct(shape, jnp.float32),
        compiler_params=params(16),
        cost_estimate=cost(size * keep.shape[1], 16 * size * keep.shape[1]),
        name="merge",
    )(keep, got, *after)


def finish_kernel(parts, samples, starts, uses, *refs):
    pieces = len(starts)
    out, body, marks, scales = refs[2 * pieces :]
    share, cols = out.shape
    total = samples * parts
    me = lax.axis_index("samp")
    upper = me >= parts // 2

    def take(i):
        keep, got = refs[2 * i], refs[2 * i + 1]
        width = keep.shape[1]
        here = slice(starts[i], starts[i] + width)
        body[:, here] = keep[:share, :] + got[:share, :]
        half = parts // 2
        stats = jnp.concatenate(
            [ref[share:, :].reshape(half, STATS, width) for ref in (keep, got)], 0
        )
        mean = jnp.sum(stats, 0, keepdims=True) / parts
        apart = (stats - mean) + pltpu.roll(stats, STATS - 2, 1)
        apart = apart - jnp.sum(apart, 0, keepdims=True) / parts
        kind = lax.broadcasted_iota(jnp.int32, stats.shape, 1)
        mark = jnp.where(kind < 2, apart, jnp.where(kind < 4, stats, 0.0))
        moved = jnp.sum(mark * mark, 0) * samples
        squares = jnp.sum(stats, 0)
        spread = (squares[4:6] + (moved[0:2] - moved[2:4])) / total
        marks[:, here] = mark.reshape(parts * STATS, width)
        scales[0:2, here] = lax.rsqrt(spread + EPS)

    for i in range(pieces):
        if uses[i] is None:
            take(i)
        else:
            pl.when(upper == uses[i])(functools.partial(take, i))
    first = me * share
    if share % 128 == 0:
        window = pl.ds(pl.multiple_of(first, 128), share)
        row_marks, row_scale = marks[:, window], scales[0:1, window]
    else:
        inside = lax.rem(first, 128)
        window = pl.ds(pl.multiple_of(first - inside, 128), 128)
        back = lax.rem(128 - inside, 128)
        row_marks = pltpu.roll(marks[:, window], back, 1)[:, :share]
        row_scale = pltpu.roll(jnp.broadcast_to(scales[0:1, window], (8, 128)), back, 1)[0:1, :share]
    row_scale = jnp.broadcast_to(row_scale, (128, share)).T / total
    kind = lax.broadcasted_iota(jnp.int32, row_marks.shape, 0) % STATS
    signed = jnp.where(kind == 0, row_marks, jnp.where(kind == 2, -row_marks, 0.0)) * samples
    signed_next = pltpu.roll(signed, 1, 0)
    dot = functools.partial(
        lax.dot_general,
        dimension_numbers=(((0,), (0,)), ((), ())),
        precision=lax.Precision.HIGHEST,
        preferred_element_type=jnp.float32,
    )
    row = first + lax.broadcasted_iota(jnp.int32, (share, 128), 0)
    lane = lax.broadcasted_iota(jnp.int32, (share, 128), 1)
    own_fix, ahead_fix = dot(signed, marks[...]), dot(signed_next, marks[...])
    for left in range(0, cols, 128):
        here = slice(left, left + 128)
        own = lane + left > row
        fix = jnp.where(own, own_fix[:, here], ahead_fix[:, here])
        scale = jnp.where(own, scales[0:1, here], scales[1:2, here])
        body[:, here] = (body[:, here] + fix) * scale * row_scale
    turned = pltpu.roll(body[...], lax.rem(2 * cols - first - 1, cols), 1)
    row = lax.broadcasted_iota(jnp.int32, (share, cols), 0)
    step = 1
    while step < share:
        moved = pltpu.roll(turned, cols - step, 1)
        turned = jnp.where((row & step) != 0, moved, turned)
        step *= 2
    out[...] = turned


def finish(parts, samples, share, cols, starts, uses, pairs):
    flat = [array for pair in pairs for array in pair]
    return pl.pallas_call(
        functools.partial(finish_kernel, parts, samples, starts, uses),
        in_specs=[VMEM] * len(flat),
        out_specs=VMEM,
        out_shape=jax.ShapeDtypeStruct((share, cols), jnp.float32),
        scratch_shapes=[
            pltpu.VMEM((share, cols), jnp.float32),
            pltpu.VMEM((parts * STATS, cols), jnp.float32),
            pltpu.VMEM((8, cols), jnp.float32),
        ],
        compiler_params=params(32),
        cost_estimate=cost(40 * share * cols, 16 * share * cols),
        name="finish",
    )(*flat)


def swap(array, bit, parts):
    return lax.ppermute(array, "samp", [(i, i ^ (1 << bit)) for i in range(parts)])


def hand_over(array, upper, parts):
    half = parts // 2
    return lax.ppermute(array, "samp", [(i, i ^ half) for i in range(parts) if (i >= half) != upper])


def local(dosages):
    samples, cols = dosages.shape
    parts = lax.axis_size("samp")
    blocks = lax.axis_size("var")
    share = cols // parts
    steps = parts.bit_length() - 1
    quarter, half = cols // 4, cols // 2
    route = [(i, i - 1) for i in range(1, blocks)]
    pieces = [
        (0, half, half, half),
        (0, cols, 0, quarter),
        (0, cols, quarter, quarter),
        (half, cols, half, quarter),
        (half, cols, half + quarter, quarter),
    ]
    uses = [False, None, None, True, True]

    first = lax.ppermute(dosages[:, :quarter], "var", route)
    prepared = prepare(dosages, quarter)
    last = prepared[-1]
    pairs = {}
    ahead = [None, first]

    def begin(i):
        nonlocal last
        piece = pieces[i]
        whole = uses[i] is None
        spots = parts if whole else parts // 2
        order = tuple(range(steps if whole else steps - 1))
        send, keep = gram(piece, spots, order, prepared, ahead[i], [last])
        last = keep
        pairs[i] = (keep, swap(send, 0, parts))

    def advance(i, step):
        nonlocal last
        top = steps - 1
        size = (pieces[i][1] - pieces[i][0]) >> step
        if step < top or uses[i] is None:
            send, keep = halve(size, pairs[i], [last])
            pairs[i] = (keep, swap(send, step, parts))
        else:
            keep = merge(size, pairs[i], [last])
            pairs[i] = (keep, hand_over(keep, uses[i], parts))
        last = keep

    begin(0)
    ahead += [
        lax.ppermute(block, "var", route) for block in cut(dosages, quarter, [last])
    ]
    plan = [(1, 0), (0, 1), (2, 0), (0, 2), (3, 0), (1, 1), (4, 0), (1, 2), (2, 1), (3, 1), (2, 2), (4, 1), (3, 2), (4, 2)]
    for i, step in plan:
        if step == 0:
            begin(i)
        elif step < steps:
            advance(i, step)
    for step in range(3, steps):
        for i in range(len(pieces)):
            advance(i, step)
    starts = [piece[2] for piece in pieces]
    return finish(parts, samples, share, cols, starts, uses, [pairs[i] for i in range(len(pieces))])


def solution(mesh):
    in_specs = (P("samp", "var"),)
    out_specs = P(("var", "samp"), None)
    return jax.shard_map(local, mesh=mesh, in_specs=in_specs, out_specs=out_specs, check_vma=False)
```

```python
import functools

import jax
import jax.numpy as jnp
from jax import lax
from jax.experimental import pallas as pl
from jax.experimental.pallas import tpu as pltpu
from jax.sharding import PartitionSpec as P

EPS = 1e-06
STATS = 8
VMEM = pl.BlockSpec(memory_space=pltpu.VMEM)
ANY = pl.BlockSpec(memory_space=pl.ANY)


def params(mib):
    return pltpu.CompilerParams(vmem_limit_bytes=mib << 20)


def cost(weight):
    return pl.CostEstimate(flops=int(weight * 1e9), bytes_accessed=1, transcendentals=0)


def split(value):
    high = value.astype(jnp.bfloat16)
    low = (value - high.astype(jnp.float32)).astype(jnp.bfloat16)
    return high, low


def centre(block):
    count = block.shape[0]
    mean = jnp.sum(block, 0, keepdims=True) / count
    centred = block - mean
    left = jnp.sum(centred, 0, keepdims=True) / count
    squares = jnp.sum(centred * centred, 0, keepdims=True)
    return centred, mean, left, squares


def prepare_kernel(dosages, high_t, low_t, stats, stats_next, *refs):
    blocks, done = refs[:-1], refs[-1]
    width = blocks[0].shape[1]
    copies = []
    for i, block in enumerate(blocks):
        taken = dosages.at[:, pl.ds(i * width, width)]
        copies.append(pltpu.make_async_copy(taken, block, done.at[i]))
    for copy in copies:
        copy.start()
    for i, block in enumerate(blocks):
        copies[i].wait()
        here = pl.ds(i * width, width)
        centred, mean, left, squares = centre(block[...])
        high_t[here, :], low_t[here, :] = split(centred.T)
        zero = jnp.zeros_like(mean)
        rows = [mean, zero, left, zero, squares, zero, zero, zero]
        stats[:, here] = jnp.concatenate(rows, 0)
        rows = [zero, mean, zero, left, zero, squares, zero, zero]
        stats_next[:, here] = jnp.concatenate(rows, 0)


def prepare(dosages, width):
    samples, cols = dosages.shape
    count = cols // width
    half_t = jax.ShapeDtypeStruct((cols, samples), jnp.bfloat16)
    stats = jax.ShapeDtypeStruct((STATS, cols), jnp.float32)
    block = jax.ShapeDtypeStruct((samples, width), jnp.float32)
    out = pl.pallas_call(
        prepare_kernel,
        in_specs=[pl.BlockSpec(memory_space=pltpu.HBM)],
        out_specs=[VMEM] * (4 + count),
        out_shape=[half_t, half_t, stats, stats] + [block] * count,
        scratch_shapes=[pltpu.SemaphoreType.DMA((count,))],
        compiler_params=params(45),
        cost_estimate=cost(4),
        name="prepare",
    )(dosages)
    return out[:4], out[4:]


def place(owner, me, order):
    apart = jnp.bitwise_xor(owner, me)
    spot = 0
    for bit in order:
        spot = spot * 2 + (lax.shift_right_logical(apart, bit) & 1)
    return spot


def product(high_t, low_t, rows, high, low, side):
    sides = (((1,), (side,)), ((), ()))
    dot = functools.partial(lax.dot_general, dimension_numbers=sides, preferred_element_type=jnp.float32)
    a, b = high_t[rows, :], low_t[rows, :]
    return dot(a, high) + (dot(a, low) + dot(b, high))


def gram_kernel(piece, spots, order, passed, high_t, low_t, *refs):
    first, last, start, width = piece
    send, keep = refs[len(refs) - 2 - passed : len(refs) - passed]
    cols = high_t.shape[0]
    share = (last - first) // spots
    half = spots // 2
    me = lax.axis_index("samp")
    here = pl.ds(start, width)
    own_high, own_low = high_t[here, :], low_t[here, :]
    if last > start:
        ahead_high, ahead_low = split(centre(refs[0][...])[0])
    tall = min(width, 2 * cols // 8)
    for top in range(first, last, tall):
        band = pl.ds(top, tall)
        if top < start + width:
            tile = product(high_t, low_t, band, own_high, own_low, 1)
        if top + tall > start:
            later = product(high_t, low_t, band, ahead_high, ahead_low, 0)
            if top >= start + width:
                tile = later
            else:
                row = lax.broadcasted_iota(jnp.int32, tile.shape, 0) + top
                col = lax.broadcasted_iota(jnp.int32, tile.shape, 1) + start
                tile = jnp.where(col > row, tile, later)
        for part in range(tall // share):
            spot = place(top // share + part, me, order)
            block = tile[part * share : (part + 1) * share]
            there = pl.ds(pl.multiple_of((spot & (half - 1)) * share, share), share)

            @pl.when(spot >= half)
            def _():
                send[there, :] = block

            @pl.when(spot < half)
            def _():
                keep[there, :] = block


def gram(piece, spots, order, prepared, ahead, after, passed, weight):
    high_t, low_t = prepared
    first, last, start, width = piece
    cols, samples = high_t.shape
    shape = ((last - first) // 2, width)
    out = jax.ShapeDtypeStruct(shape, jnp.float32)
    extra = list(ahead) + list(after)
    count = len(passed)
    return pl.pallas_call(
        functools.partial(gram_kernel, piece, spots, order, count),
        in_specs=[VMEM] * (2 + len(ahead)) + [ANY] * (len(after) + count),
        out_specs=[VMEM] * 2 + [ANY] * count,
        out_shape=[out, out] + [jax.ShapeDtypeStruct(a.shape, a.dtype) for a in passed],
        input_output_aliases={2 + len(extra) + i: 2 + i for i in range(count)},
        compiler_params=params(24),
        cost_estimate=cost(weight),
        name="gram",
    )(high_t, low_t, *extra, *passed)


def add_kernel(keep, got, *refs):
    kept = refs[-1].shape[0]
    refs[-1][...] = keep[:kept, :] + got[:kept, :]
    if keep.shape[0] > kept:
        refs[-2][...] = keep[kept:, :] + got[kept:, :]


def add(pair, parts, after, weight):
    rows, cols = pair[0].shape
    out = jax.ShapeDtypeStruct((rows // parts, cols), jnp.float32)
    return pl.pallas_call(
        add_kernel,
        in_specs=[VMEM, VMEM] + [ANY] * len(after),
        out_specs=[VMEM] * parts,
        out_shape=[out] * parts,
        compiler_params=params(16),
        cost_estimate=cost(weight),
        name="add",
    )(*pair, *after)


def join_kernel(rows, one, other, *refs):
    out = refs[-1]
    if rows == one.shape[0]:
        out[...] = one[...] + other[...]
    else:
        out[: rows // 2, :] = one[...]
        out[rows // 2 :, :] = other[...]


def join(rows, one, other, after, weight):
    cols = one.shape[1]
    return pl.pallas_call(
        functools.partial(join_kernel, rows),
        in_specs=[VMEM, VMEM] + [ANY] * len(after),
        out_specs=VMEM,
        out_shape=jax.ShapeDtypeStruct((rows, cols), jnp.float32),
        compiler_params=params(16),
        cost_estimate=cost(weight),
        name="join",
    )(one, other, *after)


def weigh_kernel(parts, samples, one, other, *refs):
    fix, factor, marks = refs[-3:]
    share, cols = fix.shape
    total = samples * parts
    me = lax.axis_index("samp")
    stats = jnp.concatenate([ref[...].reshape(parts // 2, STATS, cols) for ref in (one, other)], 0)
    mean = jnp.sum(stats, 0, keepdims=True) / parts
    apart = (stats - mean) + pltpu.roll(stats, STATS - 2, 1)
    apart = apart - jnp.sum(apart, 0, keepdims=True) / parts
    kind = lax.broadcasted_iota(jnp.int32, stats.shape, 1)
    mark = jnp.where(kind < 2, apart, jnp.where(kind < 4, stats, 0.0))
    moved = jnp.sum(mark * mark, 0) * samples
    squares = jnp.sum(stats, 0)
    spread = (squares[4:6] + (moved[0:2] - moved[2:4])) / total
    marks[: parts * STATS, :] = mark.reshape(parts * STATS, cols)
    marks[parts * STATS :, :] = jnp.concatenate([lax.rsqrt(spread + EPS)] * (STATS // 2), 0)
    first = me * share
    if share % 128 == 0:
        rows = marks[:, pl.ds(pl.multiple_of(first, 128), share)]
    else:
        inside = lax.rem(first, 128)
        window = pl.ds(pl.multiple_of(first - inside, 128), 128)
        rows = pltpu.roll(marks[:, window], lax.rem(128 - inside, 128), 1)[:, :share]
    row_scale = rows[parts * STATS : parts * STATS + 1] / total
    row_scale = jnp.broadcast_to(row_scale, (128, share)).T
    rows = rows[: parts * STATS]
    kind = lax.broadcasted_iota(jnp.int32, rows.shape, 0) % STATS
    signed = jnp.where(kind == 0, rows, jnp.where(kind == 2, -rows, 0.0)) * samples
    signed_next = pltpu.roll(signed, 1, 0)
    dot = functools.partial(
        lax.dot_general,
        dimension_numbers=(((0,), (0,)), ((), ())),
        precision=lax.Precision.HIGHEST,
        preferred_element_type=jnp.float32,
    )
    every = marks[: parts * STATS, :]
    own_fix, ahead_fix = dot(signed, every), dot(signed_next, every)
    row = first + lax.broadcasted_iota(jnp.int32, (share, 128), 0)
    lane = lax.broadcasted_iota(jnp.int32, (share, 128), 1)
    for left in range(0, cols, 128):
        here = slice(left, left + 128)
        own = lane + left > row
        scale = marks[parts * STATS : parts * STATS + 2, here]
        fix[:, here] = jnp.where(own, own_fix[:, here], ahead_fix[:, here])
        factor[:, here] = jnp.where(own, scale[0:1], scale[1:2]) * row_scale


def weigh(parts, samples, share, one, other, after, weight):
    cols = one.shape[1]
    out = jax.ShapeDtypeStruct((share, cols), jnp.float32)
    return pl.pallas_call(
        functools.partial(weigh_kernel, parts, samples),
        in_specs=[VMEM, VMEM] + [ANY] * len(after),
        out_specs=[VMEM] * 2,
        out_shape=[out, out],
        scratch_shapes=[pltpu.VMEM(((parts + 1) * STATS, cols), jnp.float32)],
        compiler_params=params(16),
        cost_estimate=cost(weight),
        name="weigh",
    )(one, other, *after)


def finish_kernel(parts, starts, uses, sizes, fix, factor, *refs):
    out, body = refs[-2:]
    share, cols = out.shape
    me = lax.axis_index("samp")
    upper = me >= parts // 2

    def take(i):
        mine = refs[sum(sizes[:i]) : sum(sizes[: i + 1])]
        total = sum(ref[...] for ref in mine)
        here = slice(starts[i], starts[i] + total.shape[1])
        body[:, here] = (total + fix[:, here]) * factor[:, here]

    for i in range(len(starts)):
        if uses[i] is None:
            take(i)
        else:
            pl.when(upper == uses[i])(functools.partial(take, i))
    first = me * share
    turned = pltpu.roll(body[...], lax.rem(2 * cols - first - 1, cols), 1)
    row = lax.broadcasted_iota(jnp.int32, (share, cols), 0)
    step = 1
    while step < share:
        moved = pltpu.roll(turned, cols - step, 1)
        turned = jnp.where((row & step) != 0, moved, turned)
        step *= 2
    out[...] = turned


def finish(parts, starts, uses, weights, sums):
    flat = [array for arrays in sums for array in arrays]
    sizes = [len(arrays) for arrays in sums]
    share, cols = weights[0].shape
    return pl.pallas_call(
        functools.partial(finish_kernel, parts, starts, uses, sizes),
        in_specs=[VMEM] * (2 + len(flat)),
        out_specs=VMEM,
        out_shape=jax.ShapeDtypeStruct((share, cols), jnp.float32),
        scratch_shapes=[pltpu.VMEM((share, cols), jnp.float32)],
        compiler_params=params(16),
        cost_estimate=cost(4),
        name="finish",
    )(*weights, *flat)


PLAN = (
    (0, 0, 2), (1, 0, 2), (0, 1, 2), (5, 0, 2), (2, 0, 2), (0, 2, 2), (1, 1, 2), (3, 0, 2),
    (5, 1, 2), (4, 0, 2), (2, 1, 2), (1, 2, 2), (5, 2, 2), (0, 3, 2), (3, 1, 2), (2, 2, 2),
    (5, 3, 2), (1, 3, 2), (4, 1, 2), (3, 2, 2), (2, 3, 2), (4, 2, 2), (3, 3, 2),
)
ORDERS = ((0, 1), (0, 1, 2), (0, 1, 2), (0, 1), (0, 1))


def plan(steps, pieces):
    tasks = [task for task in PLAN if task[1] <= steps]
    named = {task[:2] for task in tasks}
    for step in range(steps + 1):
        for i in (pieces, *range(pieces)):
            if (i, step) not in named and (step < steps or i == pieces):
                tasks.append((i, step, 2))
    return tasks


def swap(array, bit, parts):
    return lax.ppermute(array, "samp", [(i, i ^ (1 << bit)) for i in range(parts)])


def hand_over(array, upper, parts):
    half = parts // 2
    return lax.ppermute(array, "samp", [(i, i ^ half) for i in range(parts) if (i >= half) != upper])


def local(dosages):
    samples, cols = dosages.shape
    parts = lax.axis_size("samp")
    blocks = lax.axis_size("var")
    share = cols // parts
    steps = parts.bit_length() - 1
    quarter, half = cols // 4, cols // 2
    route = [(i, i - 1) for i in range(1, blocks)]
    pieces = [
        (0, half, half, half),
        (0, cols, 0, quarter),
        (0, cols, quarter, quarter),
        (half, cols, half, quarter),
        (half, cols, half + quarter, quarter),
    ]
    uses = [False, None, None, True, True]

    (high_t, low_t, stats, stats_next), cuts = prepare(dosages, quarter)
    last = stats
    pairs, sums = {}, {}
    weights = None
    passed = {(0, 0): [cuts[1], stats_next], (1, 0): [cuts[2]], (2, 0): [cuts[3]]}
    come = [None, lax.ppermute(cuts[0], "var", route)]

    def bits(i):
        whole = uses[i] is None
        used = ORDERS[i][: steps if whole else steps - 1]
        return used + tuple(range(len(used), steps if whole else steps - 1))

    for i, step, weight in plan(steps, len(pieces)):
        if i == len(pieces):
            if step == 0:
                stats_next = come.pop(3)
            if step < steps:
                stats = last = join(STATS << step, stats, stats_next, [last], weight)
                stats_next = swap(stats, step, parts)
            else:
                weights = weigh(parts, samples, share, stats, stats_next, [last], weight)
                last = weights[0]
        elif step == 0:
            piece = pieces[i]
            spots = parts if uses[i] is None else parts // 2
            near = [] if come[i] is None else [come[i]]
            held = passed.get((i, 0), [])
            send, last, *held = gram(piece, spots, bits(i), (high_t, low_t), near, [last], held, weight)
            pairs[i] = (last, swap(send, bits(i)[0], parts))
            come += [lax.ppermute(array, "var", route) for array in held]
        elif step == steps:
            (last,) = sums[i] = add(pairs[i], 1, [last], weight)
        elif step < len(bits(i)):
            send, last = add(pairs[i], 2, [last], weight)
            pairs[i] = (last, swap(send, bits(i)[step], parts))
        else:
            (last,) = add(pairs[i], 1, [last], weight)
            pairs[i] = (last, hand_over(last, uses[i], parts))
    starts = [piece[2] for piece in pieces]
    return finish(parts, starts, uses, weights, [sums.get(i, pairs[i]) for i in range(len(pieces))])


def solution(mesh):
    in_specs = (P("samp", "var"),)
    out_specs = P(("var", "samp"), None)
    return jax.shard_map(local, mesh=mesh, in_specs=in_specs, out_specs=out_specs, check_vma=False)
```

```python
import functools

import jax
import jax.numpy as jnp
from jax import lax
from jax.experimental import pallas as pl
from jax.experimental.pallas import tpu as pltpu
from jax.sharding import PartitionSpec as P

EPS = 1e-06
STATS = 8
VMEM = pl.BlockSpec(memory_space=pltpu.VMEM)
ANY = pl.BlockSpec(memory_space=pl.ANY)


def params(mib):
    return pltpu.CompilerParams(vmem_limit_bytes=mib << 20)


def cost(weight):
    return pl.CostEstimate(flops=int(weight * 1e9), bytes_accessed=1, transcendentals=0)


def split(value):
    high = value.astype(jnp.bfloat16)
    low = (value - high.astype(jnp.float32)).astype(jnp.bfloat16)
    return high, low


def centre(block):
    count = block.shape[0]
    mean = jnp.sum(block, 0, keepdims=True) / count
    centred = block - mean
    left = jnp.sum(centred, 0, keepdims=True) / count
    squares = jnp.sum(centred * centred, 0, keepdims=True)
    return centred, mean, left, squares


def prepare_kernel(dosages, high_t, low_t, stats, *refs):
    blocks, done = refs[:-1], refs[-1]
    width = blocks[0].shape[1]
    long = stats.shape[1]
    copies = []
    for i, block in enumerate(blocks):
        taken = dosages.at[:, pl.ds(i * width, width)]
        copies.append(pltpu.make_async_copy(taken, block, done.at[i]))
    for copy in copies:
        copy.start()
    for i, block in enumerate(blocks):
        copies[i].wait()
        here = pl.ds(i * width, width)
        centred, mean, left, squares = centre(block[...])
        high_t[here, :], low_t[here, :] = split(centred.T)
        rows = [mean, left, squares] + [jnp.zeros_like(mean)] * (STATS - 3)
        first = i * width // long * STATS
        stats[first : first + STATS, i * width % long : i * width % long + width] = jnp.concatenate(rows, 0)


def prepare(dosages, width, long):
    samples, cols = dosages.shape
    count = cols // width
    half_t = jax.ShapeDtypeStruct((cols, samples), jnp.bfloat16)
    stats = jax.ShapeDtypeStruct((STATS * cols // long, long), jnp.float32)
    block = jax.ShapeDtypeStruct((samples, width), jnp.float32)
    out = pl.pallas_call(
        prepare_kernel,
        in_specs=[pl.BlockSpec(memory_space=pltpu.HBM)],
        out_specs=[VMEM] * (3 + count),
        out_shape=[half_t, half_t, stats] + [block] * count,
        scratch_shapes=[pltpu.SemaphoreType.DMA((count,))],
        compiler_params=params(45),
        cost_estimate=cost(4),
        name="prepare",
    )(dosages)
    return out[:2], out[2], out[3:]


def place(owner, me, order):
    apart = jnp.bitwise_xor(owner, me)
    spot = 0
    for bit in order:
        spot = spot * 2 + (lax.shift_right_logical(apart, bit) & 1)
    return spot


def product(high_t, low_t, rows, high, low, side):
    sides = (((1,), (side,)), ((), ()))
    dot = functools.partial(lax.dot_general, dimension_numbers=sides, preferred_element_type=jnp.float32)
    a, b = high_t[rows, :], low_t[rows, :]
    return dot(a, high) + (dot(a, low) + dot(b, high))


def gram_kernel(piece, spots, order, ahead, rows, high_t, low_t, *refs):
    first, last, start, width = piece
    send, keep = refs[-2:]
    cols = high_t.shape[0]
    share = (last - first) // spots
    half = spots // 2
    me = lax.axis_index("samp")
    here = pl.ds(start, width)
    own_high, own_low = high_t[here, :], low_t[here, :]
    if rows:
        for out in (send, keep):
            out[half * share :, :] = refs[ahead][...]
    if ahead:
        ahead_high, ahead_low = split(centre(refs[0][...])[0])
    tall = min(width, 2 * cols // 8)
    for top in range(first, last, tall):
        band = pl.ds(top, tall)
        if top < start + width:
            tile = product(high_t, low_t, band, own_high, own_low, 1)
        if top + tall > start:
            later = product(high_t, low_t, band, ahead_high, ahead_low, 0)
            if top >= start + width:
                tile = later
            else:
                row = lax.broadcasted_iota(jnp.int32, tile.shape, 0) + top
                col = lax.broadcasted_iota(jnp.int32, tile.shape, 1) + start
                tile = jnp.where(col > row, tile, later)
        for part in range(tall // share):
            spot = place(top // share + part, me, order)
            block = tile[part * share : (part + 1) * share]
            there = pl.ds(pl.multiple_of((spot & (half - 1)) * share, share), share)

            @pl.when(spot >= half)
            def _():
                send[there, :] = block

            @pl.when(spot < half)
            def _():
                keep[there, :] = block


def gram(piece, spots, order, prepared, ahead, rows, after, weight):
    first, last, start, width = piece
    extra = sum(array.shape[0] for array in rows)
    out = jax.ShapeDtypeStruct(((last - first) // 2 + extra, width), jnp.float32)
    return pl.pallas_call(
        functools.partial(gram_kernel, piece, spots, order, len(ahead), extra),
        in_specs=[VMEM] * (2 + len(ahead) + len(rows)) + [ANY] * len(after),
        out_specs=[VMEM] * 2,
        out_shape=[out, out],
        compiler_params=params(24),
        cost_estimate=cost(weight),
        name="gram",
    )(*prepared, *ahead, *rows, *after)


def add_kernel(size, parts, extra, keep, got, *refs):
    out = refs[len(refs) - parts :]
    kept = size // parts
    rows = keep.shape[0] - size
    for i, ref in enumerate(out):
        here = slice((parts - 1 - i) * kept, (parts - i) * kept)
        ref[:kept, :] = keep[here, :] + got[here, :]
        if extra == rows and rows:
            far = got[size:, :].reshape(rows // STATS, STATS, -1)
            ref[kept:, :] = keep[size:, :] + pltpu.roll(far, STATS // 2, 1).reshape(rows, -1)
        elif rows:
            ref[kept : kept + rows, :] = keep[size:, :]
            ref[kept + rows :, :] = got[size:, :]


def add(size, pair, parts, extra, after, weight):
    cols = pair[0].shape[1]
    out = jax.ShapeDtypeStruct((size // parts + extra, cols), jnp.float32)
    return pl.pallas_call(
        functools.partial(add_kernel, size, parts, extra),
        in_specs=[VMEM, VMEM] + [ANY] * len(after),
        out_specs=[VMEM] * parts,
        out_shape=[out] * parts,
        compiler_params=params(16),
        cost_estimate=cost(weight),
        name="add",
    )(*pair, *after)


def part_kernel(size, keep, got, *refs):
    body, rows = refs[-2:]
    extra = keep.shape[0] - size
    body[...] = keep[:size, :] + got[:size, :]
    rows[:extra, :] = keep[size:, :]
    rows[extra:, :] = got[size:, :]


def part(size, pair, after, weight):
    rows, cols = pair[0].shape
    shapes = [(size, cols), (2 * (rows - size), cols)]
    return pl.pallas_call(
        functools.partial(part_kernel, size),
        in_specs=[VMEM, VMEM] + [ANY] * len(after),
        out_specs=[VMEM] * 2,
        out_shape=[jax.ShapeDtypeStruct(shape, jnp.float32) for shape in shapes],
        compiler_params=params(16),
        cost_estimate=cost(weight),
        name="part",
    )(*pair, *after)


def join_kernel(one, other, *refs):
    rows = one.shape[0]
    refs[-1][:rows, :] = one[...]
    refs[-1][rows:, :] = other[...]


def join(pair, after, weight):
    rows, cols = pair[0].shape
    return pl.pallas_call(
        join_kernel,
        in_specs=[VMEM, VMEM] + [ANY] * len(after),
        out_specs=VMEM,
        out_shape=jax.ShapeDtypeStruct((2 * rows, cols), jnp.float32),
        compiler_params=params(16),
        cost_estimate=cost(weight),
        name="join",
    )(*pair, *after)


def cross_kernel(parts, start, keep, got, early, *refs):
    send, mine = refs[-2:]
    total = keep[...] + got[...]
    other = early[:, start : start + total.shape[1]]
    upper = lax.axis_index("samp") >= parts // 2

    @pl.when(upper)
    def _():
        send[...] = other
        mine[...] = total

    @pl.when(jnp.logical_not(upper))
    def _():
        send[...] = total
        mine[...] = other


def cross(parts, start, pair, early, after, weight):
    out = jax.ShapeDtypeStruct(pair[0].shape, jnp.float32)
    return pl.pallas_call(
        functools.partial(cross_kernel, parts, start),
        in_specs=[VMEM] * 3 + [ANY] * len(after),
        out_specs=[VMEM] * 2,
        out_shape=[out, out],
        compiler_params=params(16),
        cost_estimate=cost(weight),
        name="cross",
    )(*pair, early, *after)


def weigh_kernel(parts, samples, own, ahead, *refs):
    fix, factor, marks = refs[-3:]
    share, cols = fix.shape
    total = samples * parts
    height = parts * STATS // 2
    me = lax.axis_index("samp")
    long = own.shape[1]

    def every(value):
        value = jnp.sum(value, 0)
        return value + pltpu.roll(value, STATS // 2, 0)

    for side, ref in enumerate((own, ahead)):
        pairs = ref[...].reshape(parts // 2, cols // long, STATS, long)
        for i in range(cols // long):
            stats = pairs[:, i]
            apart = (stats - every(stats)[None] / parts) + pltpu.roll(stats, STATS - 1, 1)
            apart = apart - every(apart)[None] / parts
            kind = lax.broadcasted_iota(jnp.int32, stats.shape, 1) % (STATS // 2)
            mark = jnp.where(kind == 0, apart, jnp.where(kind == 1, stats, 0.0))
            moved = every(mark * mark) * samples
            squares = every(stats)
            spread = (squares[2:3] + (moved[0:1] - moved[1:2])) / total
            here = slice(i * long, (i + 1) * long)
            marks[side * height : (side + 1) * height, here] = mark.reshape(height, long)
            place = 2 * height + side * STATS
            marks[place : place + STATS, here] = jnp.broadcast_to(lax.rsqrt(spread + EPS), (STATS, long))
    first = me * share
    if share % 128 == 0:
        rows = marks[:, pl.ds(pl.multiple_of(first, 128), share)]
    else:
        inside = lax.rem(first, 128)
        window = pl.ds(pl.multiple_of(first - inside, 128), 128)
        rows = pltpu.roll(marks[:, window], lax.rem(128 - inside, 128), 1)[:, :share]
    row_scale = rows[2 * height : 2 * height + 1] / total
    row_scale = jnp.broadcast_to(row_scale, (128, share)).T
    rows = rows[:height]
    kind = lax.broadcasted_iota(jnp.int32, rows.shape, 0) % (STATS // 2)
    signed = jnp.where(kind == 0, rows, jnp.where(kind == 1, -rows, 0.0)) * samples
    dot = functools.partial(
        lax.dot_general,
        dimension_numbers=(((0,), (0,)), ((), ())),
        precision=lax.Precision.HIGHEST,
        preferred_element_type=jnp.float32,
    )
    own_fix, ahead_fix = dot(signed, marks[:height, :]), dot(signed, marks[height : 2 * height, :])
    row = first + lax.broadcasted_iota(jnp.int32, (share, 128), 0)
    lane = lax.broadcasted_iota(jnp.int32, (share, 128), 1)
    for left in range(0, cols, 128):
        here = slice(left, left + 128)
        mine = lane + left > row
        own_scale = marks[2 * height : 2 * height + 1, here]
        ahead_scale = marks[2 * height + STATS : 2 * height + STATS + 1, here]
        fix[:, here] = jnp.where(mine, own_fix[:, here], ahead_fix[:, here])
        factor[:, here] = jnp.where(mine, own_scale, ahead_scale) * row_scale


def weigh(parts, samples, share, cols, own, ahead, after, weight):
    out = jax.ShapeDtypeStruct((share, cols), jnp.float32)
    return pl.pallas_call(
        functools.partial(weigh_kernel, parts, samples),
        in_specs=[VMEM, VMEM] + [ANY] * len(after),
        out_specs=[VMEM] * 2,
        out_shape=[out, out],
        scratch_shapes=[pltpu.VMEM(((parts + 2) * STATS, cols), jnp.float32)],
        compiler_params=params(16),
        cost_estimate=cost(weight),
        name="weigh",
    )(own, ahead, *after)


def finish_kernel(starts, sizes, fix, factor, *refs):
    out, body = refs[-2:]
    share, cols = out.shape
    me = lax.axis_index("samp")
    for i, start in enumerate(starts):
        mine = refs[sum(sizes[:i]) : sum(sizes[: i + 1])]
        total = sum(ref[...] for ref in mine)
        here = slice(start, start + total.shape[1])
        body[:, here] = (total + fix[:, here]) * factor[:, here]
    first = me * share
    turned = pltpu.roll(body[...], lax.rem(2 * cols - first - 1, cols), 1)
    row = lax.broadcasted_iota(jnp.int32, (share, cols), 0)
    step = 1
    while step < share:
        moved = pltpu.roll(turned, cols - step, 1)
        turned = jnp.where((row & step) != 0, moved, turned)
        step *= 2
    out[...] = turned


def finish(starts, weights, sums):
    flat = [array for arrays in sums for array in arrays]
    sizes = [len(arrays) for arrays in sums]
    share, cols = weights[0].shape
    return pl.pallas_call(
        functools.partial(finish_kernel, starts, sizes),
        in_specs=[VMEM] * (2 + len(flat)),
        out_specs=VMEM,
        out_shape=jax.ShapeDtypeStruct((share, cols), jnp.float32),
        scratch_shapes=[pltpu.VMEM((share, cols), jnp.float32)],
        compiler_params=params(16),
        cost_estimate=cost(4),
        name="finish",
    )(*weights, *flat)


PLAN = (
    (0, 0, 0.01),
    (1, 0, 0.01),
    (0, 1, 0.01),
    (2, 0, 0.01),
    (0, 2, 0.01),
    (1, 1, 0.01),
    (5, 0, 1.8),
    (3, 0, 0.01),
    (1, 2, 0.01),
    (2, 1, 0.01),
    (4, 0, 0.01),
    (3, 1, 0.01),
    (1, 3, 2.5),
    (2, 2, 0.01),
    (4, 1, 0.01),
    (3, 2, 2.5),
    (4, 2, 0.01),
    (5, 1, 0.01),
    (2, 3, 1.6),
    (3, 3, 0.08),
)


def plan(steps, pieces):
    if steps == 3:
        return PLAN
    tasks = [(i, step, 1) for step in range(steps) for i in range(pieces)]
    return tasks + [(pieces, 0, 1), (pieces, 1, 1)]


def swap(array, bit, parts):
    return lax.ppermute(array, "samp", [(i, i ^ (1 << bit)) for i in range(parts)])


def local(dosages):
    samples, cols = dosages.shape
    parts = lax.axis_size("samp")
    blocks = lax.axis_size("var")
    share = cols // parts
    steps = parts.bit_length() - 1
    quarter, half = cols // 4, cols // 2
    route = [(i, i - 1) for i in range(1, blocks)]
    pieces = [
        (0, half, half, half),
        (0, cols, 0, quarter),
        (0, cols, quarter, quarter),
        (half, cols, half, quarter),
        (half, cols, half + quarter, quarter),
    ]
    prepared, stats, cuts = prepare(dosages, quarter, half)
    last = stats
    come = [[]] + [[lax.ppermute(cut, "var", route)] for cut in cuts]
    pairs, sums = {}, {}

    for i, step, weight in plan(steps, len(pieces)):
        after = [last]
        if i == len(pieces) and step == 0:
            stats = last = join(stats, after, weight)
            stats_next = lax.ppermute(stats, "var", route)
            continue
        if i == len(pieces):
            weights = weigh(parts, samples, share, cols, stats, stats_next, after, weight)
            last = weights[0]
            continue
        first, end, start, width = pieces[i]
        spots = parts * (end - first) // cols
        order = tuple(range(spots.bit_length() - 1))
        size = (end - first) >> step
        if step == 0:
            rows = [stats] if i == 0 else []
            send, last = gram(pieces[i], spots, order, prepared, come[i], rows, after, weight)
        elif step < steps - 1:
            rows = pairs[i][0].shape[0] - size
            send, last = add(size, pairs[i], 2, rows if step == 1 else 2 * rows, after, weight)
        elif step == steps:
            (last,) = sums[i] = add(share, pairs[i], 1, 0, after, weight)
            continue
        elif i == 0:
            pairs[i], stats = part(share, pairs[i], after, weight)
            last = pairs[i]
            stats = (stats, swap(stats, step, parts))
            continue
        elif end - first == cols:
            send, last = add(size, pairs[i], 2, 0, after, weight)
        else:
            send, last = cross(parts, start - half, pairs[i], pairs[0], after, weight)
        pairs[i] = (last, swap(send, step, parts))
    kept = range(1, len(pieces))
    return finish([pieces[i][2] for i in kept], weights, [sums.get(i, pairs[i]) for i in kept])


def solution(mesh):
    in_specs = (P("samp", "var"),)
    out_specs = P(("var", "samp"), None)
    return jax.shard_map(local, mesh=mesh, in_specs=in_specs, out_specs=out_specs, check_vma=False)
```

```python
import functools

import jax
import jax.numpy as jnp
from jax import lax
from jax.experimental import pallas as pl
from jax.experimental.pallas import tpu as pltpu
from jax.sharding import PartitionSpec as P

EPS = 1e-06
STATS = 8
VMEM = pl.BlockSpec(memory_space=pltpu.VMEM)
ANY = pl.BlockSpec(memory_space=pl.ANY)


def params(mib):
    return pltpu.CompilerParams(vmem_limit_bytes=mib << 20)


def cost(weight):
    return pl.CostEstimate(flops=int(weight * 1e9), bytes_accessed=1, transcendentals=0)


def split(value):
    high = value.astype(jnp.bfloat16)
    low = (value - high.astype(jnp.float32)).astype(jnp.bfloat16)
    return high, low


def centre(block):
    count = block.shape[0]
    mean = jnp.sum(block, 0, keepdims=True) / count
    centred = block - mean
    left = jnp.sum(centred, 0, keepdims=True) / count
    squares = jnp.sum(centred * centred, 0, keepdims=True)
    return centred, mean, left, squares


def prepare_kernel(dosages, high_t, low_t, stats, *refs):
    blocks, done = refs[:-1], refs[-1]
    width = blocks[0].shape[1]
    long = stats.shape[1]
    copies = []
    for i, block in enumerate(blocks):
        taken = dosages.at[:, pl.ds(i * width, width)]
        copies.append(pltpu.make_async_copy(taken, block, done.at[i]))
    for copy in copies:
        copy.start()
    for i, block in enumerate(blocks):
        copies[i].wait()
        here = pl.ds(i * width, width)
        centred, mean, left, squares = centre(block[...])
        high_t[here, :], low_t[here, :] = split(centred.T)
        rows = [mean, left, squares] + [jnp.zeros_like(mean)] * (STATS - 3)
        first = i * width // long * STATS
        stats[first : first + STATS, i * width % long : i * width % long + width] = jnp.concatenate(rows, 0)


def prepare(dosages, width, long):
    samples, cols = dosages.shape
    count = cols // width
    half_t = jax.ShapeDtypeStruct((cols, samples), jnp.bfloat16)
    stats = jax.ShapeDtypeStruct((STATS * cols // long, long), jnp.float32)
    block = jax.ShapeDtypeStruct((samples, width), jnp.float32)
    out = pl.pallas_call(
        prepare_kernel,
        in_specs=[pl.BlockSpec(memory_space=pltpu.HBM)],
        out_specs=[VMEM] * (3 + count),
        out_shape=[half_t, half_t, stats] + [block] * count,
        scratch_shapes=[pltpu.SemaphoreType.DMA((count,))],
        compiler_params=params(45),
        cost_estimate=cost(4),
        name="prepare",
    )(dosages)
    return out[:2], out[2], out[3:]


def place(owner, me, order):
    apart = jnp.bitwise_xor(owner, me)
    spot = 0
    for bit in order:
        spot = spot * 2 + (lax.shift_right_logical(apart, bit) & 1)
    return spot


def product(high_t, low_t, rows, high, low, side):
    sides = (((1,), (side,)), ((), ()))
    dot = functools.partial(lax.dot_general, dimension_numbers=sides, preferred_element_type=jnp.float32)
    a, b = high_t[rows, :], low_t[rows, :]
    return dot(a, high) + (dot(a, low) + dot(b, high))


def gram_kernel(piece, spots, order, ahead, rows, high_t, low_t, *refs):
    first, last, start, width = piece
    send, keep = refs[-2:]
    cols = high_t.shape[0]
    share = (last - first) // spots
    half = spots // 2
    me = lax.axis_index("samp")
    here = pl.ds(start, width)
    own_high, own_low = high_t[here, :], low_t[here, :]
    if rows:
        for out in (send, keep):
            out[half * share :, :] = refs[ahead][...]
    if ahead:
        ahead_high, ahead_low = split(centre(refs[0][...])[0])
    tall = min(width, 2 * cols // 8)
    for top in range(first, last, tall):
        band = pl.ds(top, tall)
        if top < start + width:
            tile = product(high_t, low_t, band, own_high, own_low, 1)
        if top + tall > start:
            later = product(high_t, low_t, band, ahead_high, ahead_low, 0)
            if top >= start + width:
                tile = later
            else:
                row = lax.broadcasted_iota(jnp.int32, tile.shape, 0) + top
                col = lax.broadcasted_iota(jnp.int32, tile.shape, 1) + start
                tile = jnp.where(col > row, tile, later)
        for part in range(tall // share):
            spot = place(top // share + part, me, order)
            block = tile[part * share : (part + 1) * share]
            there = pl.ds(pl.multiple_of((spot & (half - 1)) * share, share), share)

            @pl.when(spot >= half)
            def _():
                send[there, :] = block

            @pl.when(spot < half)
            def _():
                keep[there, :] = block


def gram(piece, spots, order, prepared, ahead, rows, after, weight):
    first, last, start, width = piece
    extra = sum(array.shape[0] for array in rows)
    out = jax.ShapeDtypeStruct(((last - first) // 2 + extra, width), jnp.float32)
    return pl.pallas_call(
        functools.partial(gram_kernel, piece, spots, order, len(ahead), extra),
        in_specs=[VMEM] * (2 + len(ahead) + len(rows)) + [ANY] * len(after),
        out_specs=[VMEM] * 2,
        out_shape=[out, out],
        compiler_params=params(24),
        cost_estimate=cost(weight),
        name="gram",
    )(*prepared, *ahead, *rows, *after)


def add_kernel(size, parts, extra, keep, got, *refs):
    out = refs[len(refs) - parts :]
    kept = size // parts
    rows = keep.shape[0] - size
    for i, ref in enumerate(out):
        here = slice((parts - 1 - i) * kept, (parts - i) * kept)
        ref[:kept, :] = keep[here, :] + got[here, :]
        if extra == rows and rows:
            far = got[size:, :].reshape(rows // STATS, STATS, -1)
            ref[kept:, :] = keep[size:, :] + pltpu.roll(far, STATS // 2, 1).reshape(rows, -1)
        elif rows:
            ref[kept : kept + rows, :] = keep[size:, :]
            ref[kept + rows :, :] = got[size:, :]


def add(size, pair, parts, extra, after, weight):
    cols = pair[0].shape[1]
    out = jax.ShapeDtypeStruct((size // parts + extra, cols), jnp.float32)
    return pl.pallas_call(
        functools.partial(add_kernel, size, parts, extra),
        in_specs=[VMEM, VMEM] + [ANY] * len(after),
        out_specs=[VMEM] * parts,
        out_shape=[out] * parts,
        compiler_params=params(16),
        cost_estimate=cost(weight),
        name="add",
    )(*pair, *after)


def part_kernel(size, keep, got, *refs):
    body, rows = refs[-2:]
    extra = keep.shape[0] - size
    body[...] = keep[:size, :] + got[:size, :]
    rows[:extra, :] = keep[size:, :]
    rows[extra:, :] = got[size:, :]


def part(size, pair, after, weight):
    rows, cols = pair[0].shape
    shapes = [(size, cols), (2 * (rows - size), cols)]
    return pl.pallas_call(
        functools.partial(part_kernel, size),
        in_specs=[VMEM, VMEM] + [ANY] * len(after),
        out_specs=[VMEM] * 2,
        out_shape=[jax.ShapeDtypeStruct(shape, jnp.float32) for shape in shapes],
        compiler_params=params(16),
        cost_estimate=cost(weight),
        name="part",
    )(*pair, *after)


def join_kernel(one, other, *refs):
    rows = one.shape[0]
    refs[-1][:rows, :] = one[...]
    refs[-1][rows:, :] = other[...]


def join(pair, after, weight):
    rows, cols = pair[0].shape
    return pl.pallas_call(
        join_kernel,
        in_specs=[VMEM, VMEM] + [ANY] * len(after),
        out_specs=VMEM,
        out_shape=jax.ShapeDtypeStruct((2 * rows, cols), jnp.float32),
        compiler_params=params(16),
        cost_estimate=cost(weight),
        name="join",
    )(*pair, *after)


def cross_kernel(parts, start, keep, got, early, *refs):
    send, mine = refs[-2:]
    total = keep[...] + got[...]
    other = early[:, start : start + total.shape[1]]
    upper = lax.axis_index("samp") >= parts // 2

    @pl.when(upper)
    def _():
        send[...] = other
        mine[...] = total

    @pl.when(jnp.logical_not(upper))
    def _():
        send[...] = total
        mine[...] = other


def cross(parts, start, pair, early, after, weight):
    out = jax.ShapeDtypeStruct(pair[0].shape, jnp.float32)
    return pl.pallas_call(
        functools.partial(cross_kernel, parts, start),
        in_specs=[VMEM] * 3 + [ANY] * len(after),
        out_specs=[VMEM] * 2,
        out_shape=[out, out],
        compiler_params=params(16),
        cost_estimate=cost(weight),
        name="cross",
    )(*pair, early, *after)


def weigh_kernel(parts, samples, own, ahead, *refs):
    fix, factor, marks = refs[-3:]
    share, cols = fix.shape
    total = samples * parts
    height = parts * STATS // 2
    me = lax.axis_index("samp")
    long = own.shape[1]

    def every(value):
        value = jnp.sum(value, 0)
        return value + pltpu.roll(value, STATS // 2, 0)

    for side, ref in enumerate((own, ahead)):
        pairs = ref[...].reshape(parts // 2, cols // long, STATS, long)
        for i in range(cols // long):
            stats = pairs[:, i]
            apart = (stats - every(stats)[None] / parts) + pltpu.roll(stats, STATS - 1, 1)
            apart = apart - every(apart)[None] / parts
            kind = lax.broadcasted_iota(jnp.int32, stats.shape, 1) % (STATS // 2)
            mark = jnp.where(kind == 0, apart, jnp.where(kind == 1, stats, 0.0))
            moved = every(mark * mark) * samples
            squares = every(stats)
            spread = (squares[2:3] + (moved[0:1] - moved[1:2])) / total
            here = slice(i * long, (i + 1) * long)
            marks[side * height : (side + 1) * height, here] = mark.reshape(height, long)
            place = 2 * height + side * STATS
            marks[place : place + STATS, here] = jnp.broadcast_to(lax.rsqrt(spread + EPS), (STATS, long))
    first = me * share
    if share % 128 == 0:
        rows = marks[:, pl.ds(pl.multiple_of(first, 128), share)]
    else:
        inside = lax.rem(first, 128)
        window = pl.ds(pl.multiple_of(first - inside, 128), 128)
        rows = pltpu.roll(marks[:, window], lax.rem(128 - inside, 128), 1)[:, :share]
    row_scale = rows[2 * height : 2 * height + 1] / total
    row_scale = jnp.broadcast_to(row_scale, (128, share)).T
    rows = rows[:height]
    kind = lax.broadcasted_iota(jnp.int32, rows.shape, 0) % (STATS // 2)
    signed = jnp.where(kind == 0, rows, jnp.where(kind == 1, -rows, 0.0)) * samples
    dot = functools.partial(
        lax.dot_general,
        dimension_numbers=(((0,), (0,)), ((), ())),
        precision=lax.Precision.HIGHEST,
        preferred_element_type=jnp.float32,
    )
    own_fix, ahead_fix = dot(signed, marks[:height, :]), dot(signed, marks[height : 2 * height, :])
    row = first + lax.broadcasted_iota(jnp.int32, (share, 128), 0)
    lane = lax.broadcasted_iota(jnp.int32, (share, 128), 1)
    for left in range(0, cols, 128):
        here = slice(left, left + 128)
        mine = lane + left > row
        own_scale = marks[2 * height : 2 * height + 1, here]
        ahead_scale = marks[2 * height + STATS : 2 * height + STATS + 1, here]
        fix[:, here] = jnp.where(mine, own_fix[:, here], ahead_fix[:, here])
        factor[:, here] = jnp.where(mine, own_scale, ahead_scale) * row_scale


def weigh(parts, samples, share, cols, own, ahead, after, weight):
    out = jax.ShapeDtypeStruct((share, cols), jnp.float32)
    return pl.pallas_call(
        functools.partial(weigh_kernel, parts, samples),
        in_specs=[VMEM, VMEM] + [ANY] * len(after),
        out_specs=[VMEM] * 2,
        out_shape=[out, out],
        scratch_shapes=[pltpu.VMEM(((parts + 2) * STATS, cols), jnp.float32)],
        compiler_params=params(16),
        cost_estimate=cost(weight),
        name="weigh",
    )(own, ahead, *after)


def finish_kernel(starts, sizes, fix, factor, *refs):
    out, body = refs[-2:]
    share, cols = out.shape
    first = lax.axis_index("samp") * share
    inside = lax.rem(first, 128)
    for i, start in enumerate(starts):
        mine = refs[sum(sizes[:i]) : sum(sizes[: i + 1])]
        for left in range(0, mine[0].shape[1], 128):
            total = sum(ref[:, left : left + 128] for ref in mine)
            here = slice(start + left, start + left + 128)
            there = lax.rem(start + left + cols - (first - inside), cols)
            there = pl.ds(pl.multiple_of(there, 128), 128)
            body[:, there] = (total + fix[:, here]) * factor[:, here]
    if share % 128:
        body[...] = pltpu.roll(body[...], lax.rem(cols - inside, cols), 1)
    tops = range(0, share, 8)
    turned = jnp.concatenate([pltpu.roll(body[top : top + 8, :], cols - top - 1, 1) for top in tops], 0)
    row = lax.broadcasted_iota(jnp.int32, (share, cols), 0)
    for step in (1, 2, 4):
        turned = jnp.where((row & step) != 0, pltpu.roll(turned, cols - step, 1), turned)
    out[...] = turned


def finish(starts, weights, sums):
    flat = [array for arrays in sums for array in arrays]
    sizes = [len(arrays) for arrays in sums]
    share, cols = weights[0].shape
    return pl.pallas_call(
        functools.partial(finish_kernel, starts, sizes),
        in_specs=[VMEM] * (2 + len(flat)),
        out_specs=VMEM,
        out_shape=jax.ShapeDtypeStruct((share, cols), jnp.float32),
        scratch_shapes=[pltpu.VMEM((share, cols), jnp.float32)],
        compiler_params=params(16),
        cost_estimate=cost(4),
        name="finish",
    )(*weights, *flat)


PLAN = (
    (0, 0, 0.01),
    (1, 0, 0.01),
    (0, 1, 0.01),
    (2, 0, 0.01),
    (0, 2, 0.01),
    (1, 1, 0.01),
    (5, 0, 1.8),
    (3, 0, 0.01),
    (2, 1, 0.01),
    (1, 2, 0.01),
    (4, 0, 0.01),
    (3, 1, 0.01),
    (1, 3, 0.6),
    (2, 2, 1.66),
    (4, 1, 0.01),
    (3, 2, 2.5),
    (4, 2, 0.01),
    (5, 1, 0.01),
    (2, 3, 1.6),
    (3, 3, 0.08),
)


def plan(steps, pieces):
    if steps == 3:
        return PLAN
    tasks = [(i, step, 1) for step in range(steps) for i in range(pieces)]
    return tasks + [(pieces, 0, 1), (pieces, 1, 1)]


def swap(array, bit, parts):
    return lax.ppermute(array, "samp", [(i, i ^ (1 << bit)) for i in range(parts)])


def local(dosages):
    samples, cols = dosages.shape
    parts = lax.axis_size("samp")
    blocks = lax.axis_size("var")
    share = cols // parts
    steps = parts.bit_length() - 1
    quarter, half = cols // 4, cols // 2
    route = [(i, i - 1) for i in range(1, blocks)]
    pieces = [
        (0, half, half, half),
        (0, cols, 0, quarter),
        (0, cols, quarter, quarter),
        (half, cols, half, quarter),
        (half, cols, half + quarter, quarter),
    ]
    prepared, stats, cuts = prepare(dosages, quarter, half)
    last = stats
    come = [[]] + [[lax.ppermute(cut, "var", route)] for cut in cuts]
    pairs, sums = {}, {}

    for i, step, weight in plan(steps, len(pieces)):
        after = [last]
        if i == len(pieces) and step == 0:
            stats = last = join(stats, after, weight)
            stats_next = lax.ppermute(stats, "var", route)
            continue
        if i == len(pieces):
            weights = weigh(parts, samples, share, cols, stats, stats_next, after, weight)
            last = weights[0]
            continue
        first, end, start, width = pieces[i]
        spots = parts * (end - first) // cols
        order = tuple(range(spots.bit_length() - 1))
        size = (end - first) >> step
        if step == 0:
            rows = [stats] if i == 0 else []
            send, last = gram(pieces[i], spots, order, prepared, come[i], rows, after, weight)
        elif step < steps - 1:
            rows = pairs[i][0].shape[0] - size
            send, last = add(size, pairs[i], 2, rows if step == 1 else 2 * rows, after, weight)
        elif step == steps:
            (last,) = sums[i] = add(share, pairs[i], 1, 0, after, weight)
            continue
        elif i == 0:
            pairs[i], stats = part(share, pairs[i], after, weight)
            last = pairs[i]
            stats = (stats, swap(stats, step, parts))
            continue
        elif end - first == cols:
            send, last = add(size, pairs[i], 2, 0, after, weight)
        else:
            send, last = cross(parts, start - half, pairs[i], pairs[0], after, weight)
        pairs[i] = (last, swap(send, step, parts))
    kept = range(1, len(pieces))
    return finish([pieces[i][2] for i in kept], weights, [sums.get(i, pairs[i]) for i in kept])


def solution(mesh):
    in_specs = (P("samp", "var"),)
    out_specs = P(("var", "samp"), None)
    return jax.shard_map(local, mesh=mesh, in_specs=in_specs, out_specs=out_specs, check_vma=False)
```

```python
import functools

import jax
import jax.numpy as jnp
from jax import lax
from jax.experimental import pallas as pl
from jax.experimental.pallas import tpu as pltpu
from jax.sharding import PartitionSpec as P

EPS = 1e-06
STATS = 8
VMEM = pl.BlockSpec(memory_space=pltpu.VMEM)
ANY = pl.BlockSpec(memory_space=pl.ANY)


def params(mib):
    return pltpu.CompilerParams(vmem_limit_bytes=mib << 20)


def cost(weight):
    return pl.CostEstimate(flops=int(weight * 1e9), bytes_accessed=1, transcendentals=0)


def split(value):
    high = value.astype(jnp.bfloat16)
    low = (value - high.astype(jnp.float32)).astype(jnp.bfloat16)
    return high, low


def centre(block):
    count = block.shape[0]
    mean = jnp.sum(block, 0, keepdims=True) / count
    centred = block - mean
    left = jnp.sum(centred, 0, keepdims=True) / count
    squares = jnp.sum(centred * centred, 0, keepdims=True)
    return centred, mean, left, squares


def prepare_kernel(dosages, high_t, low_t, stats, *refs):
    blocks, done = refs[:-1], refs[-1]
    width = blocks[0].shape[1]
    long = stats.shape[1]
    copies = []
    for i, block in enumerate(blocks):
        taken = dosages.at[:, pl.ds(i * width, width)]
        copies.append(pltpu.make_async_copy(taken, block, done.at[i]))
    for copy in copies:
        copy.start()
    for i, block in enumerate(blocks):
        copies[i].wait()
        here = pl.ds(i * width, width)
        centred, mean, left, squares = centre(block[...])
        high_t[here, :], low_t[here, :] = split(centred.T)
        rows = [mean, left, squares] + [jnp.zeros_like(mean)] * (STATS - 3)
        first = i * width // long * STATS
        stats[first : first + STATS, i * width % long : i * width % long + width] = jnp.concatenate(rows, 0)


def prepare(dosages, width, long):
    samples, cols = dosages.shape
    count = cols // width
    half_t = jax.ShapeDtypeStruct((cols, samples), jnp.bfloat16)
    stats = jax.ShapeDtypeStruct((STATS * cols // long, long), jnp.float32)
    block = jax.ShapeDtypeStruct((samples, width), jnp.float32)
    out = pl.pallas_call(
        prepare_kernel,
        in_specs=[pl.BlockSpec(memory_space=pltpu.HBM)],
        out_specs=[VMEM] * (3 + count),
        out_shape=[half_t, half_t, stats] + [block] * count,
        scratch_shapes=[pltpu.SemaphoreType.DMA((count,))],
        compiler_params=params(45),
        cost_estimate=cost(4),
        name="prepare",
    )(dosages)
    return out[:2], out[2], out[3:]


def place(owner, me, order):
    apart = jnp.bitwise_xor(owner, me)
    spot = 0
    for bit in order:
        spot = spot * 2 + (lax.shift_right_logical(apart, bit) & 1)
    return spot


def product(high_t, low_t, rows, high, low, side):
    sides = (((1,), (side,)), ((), ()))
    dot = functools.partial(lax.dot_general, dimension_numbers=sides, preferred_element_type=jnp.float32)
    a, b = high_t[rows, :], low_t[rows, :]
    return dot(a, high) + (dot(a, low) + dot(b, high))


def gram_kernel(piece, spots, order, ahead, rows, high_t, low_t, *refs):
    first, last, start, width = piece
    send, keep = refs[-2:]
    cols = high_t.shape[0]
    share = (last - first) // spots
    half = spots // 2
    me = lax.axis_index("samp")
    here = pl.ds(start, width)
    own_high, own_low = high_t[here, :], low_t[here, :]
    if rows:
        for out in (send, keep):
            out[half * share :, :] = refs[ahead][...]
    if ahead:
        ahead_high, ahead_low = split(centre(refs[0][...])[0])
    tall = min(width, 2 * cols // 8)
    for top in range(first, last, tall):
        band = pl.ds(top, tall)
        if top < start + width:
            tile = product(high_t, low_t, band, own_high, own_low, 1)
        if top + tall > start:
            later = product(high_t, low_t, band, ahead_high, ahead_low, 0)
            if top >= start + width:
                tile = later
            else:
                row = lax.broadcasted_iota(jnp.int32, tile.shape, 0) + top
                col = lax.broadcasted_iota(jnp.int32, tile.shape, 1) + start
                tile = jnp.where(col > row, tile, later)
        for part in range(tall // share):
            spot = place(top // share + part, me, order)
            block = tile[part * share : (part + 1) * share]
            there = pl.ds(pl.multiple_of((spot & (half - 1)) * share, share), share)

            @pl.when(spot >= half)
            def _():
                send[there, :] = block

            @pl.when(spot < half)
            def _():
                keep[there, :] = block


def gram(piece, spots, order, prepared, ahead, rows, after, weight):
    first, last, start, width = piece
    extra = sum(array.shape[0] for array in rows)
    out = jax.ShapeDtypeStruct(((last - first) // 2 + extra, width), jnp.float32)
    return pl.pallas_call(
        functools.partial(gram_kernel, piece, spots, order, len(ahead), extra),
        in_specs=[VMEM] * (2 + len(ahead) + len(rows)) + [ANY] * len(after),
        out_specs=[VMEM] * 2,
        out_shape=[out, out],
        compiler_params=params(24),
        cost_estimate=cost(weight),
        name="gram",
    )(*prepared, *ahead, *rows, *after)


def add_kernel(size, parts, extra, keep, got, *refs):
    out = refs[len(refs) - parts :]
    kept = size // parts
    rows = keep.shape[0] - size
    for i, ref in enumerate(out):
        here = slice((parts - 1 - i) * kept, (parts - i) * kept)
        ref[:kept, :] = keep[here, :] + got[here, :]
        if extra == rows and rows:
            far = got[size:, :].reshape(rows // STATS, STATS, -1)
            ref[kept:, :] = keep[size:, :] + pltpu.roll(far, STATS // 2, 1).reshape(rows, -1)
        elif rows:
            ref[kept : kept + rows, :] = keep[size:, :]
            ref[kept + rows :, :] = got[size:, :]


def add(size, pair, parts, extra, after, weight):
    cols = pair[0].shape[1]
    out = jax.ShapeDtypeStruct((size // parts + extra, cols), jnp.float32)
    return pl.pallas_call(
        functools.partial(add_kernel, size, parts, extra),
        in_specs=[VMEM, VMEM] + [ANY] * len(after),
        out_specs=[VMEM] * parts,
        out_shape=[out] * parts,
        compiler_params=params(16),
        cost_estimate=cost(weight),
        name="add",
    )(*pair, *after)


def part_kernel(size, keep, got, *refs):
    body, rows = refs[-2:]
    extra = keep.shape[0] - size
    body[...] = keep[:size, :] + got[:size, :]
    rows[:extra, :] = keep[size:, :]
    rows[extra:, :] = got[size:, :]


def part(size, pair, after, weight):
    rows, cols = pair[0].shape
    shapes = [(size, cols), (2 * (rows - size), cols)]
    return pl.pallas_call(
        functools.partial(part_kernel, size),
        in_specs=[VMEM, VMEM] + [ANY] * len(after),
        out_specs=[VMEM] * 2,
        out_shape=[jax.ShapeDtypeStruct(shape, jnp.float32) for shape in shapes],
        compiler_params=params(16),
        cost_estimate=cost(weight),
        name="part",
    )(*pair, *after)


def join_kernel(one, other, *refs):
    rows = one.shape[0]
    refs[-1][:rows, :] = one[...]
    refs[-1][rows:, :] = other[...]


def join(pair, after, weight):
    rows, cols = pair[0].shape
    return pl.pallas_call(
        join_kernel,
        in_specs=[VMEM, VMEM] + [ANY] * len(after),
        out_specs=VMEM,
        out_shape=jax.ShapeDtypeStruct((2 * rows, cols), jnp.float32),
        compiler_params=params(16),
        cost_estimate=cost(weight),
        name="join",
    )(*pair, *after)


def cross_kernel(parts, start, keep, got, early, *refs):
    send, mine = refs[-2:]
    total = keep[...] + got[...]
    other = early[:, start : start + total.shape[1]]
    upper = lax.axis_index("samp") >= parts // 2

    @pl.when(upper)
    def _():
        send[...] = other
        mine[...] = total

    @pl.when(jnp.logical_not(upper))
    def _():
        send[...] = total
        mine[...] = other


def cross(parts, start, pair, early, after, weight):
    out = jax.ShapeDtypeStruct(pair[0].shape, jnp.float32)
    return pl.pallas_call(
        functools.partial(cross_kernel, parts, start),
        in_specs=[VMEM] * 3 + [ANY] * len(after),
        out_specs=[VMEM] * 2,
        out_shape=[out, out],
        compiler_params=params(16),
        cost_estimate=cost(weight),
        name="cross",
    )(*pair, early, *after)


def weigh_kernel(parts, samples, own, ahead, *refs):
    fix, factor, marks = refs[-3:]
    share, cols = fix.shape
    total = samples * parts
    height = parts * STATS // 2
    me = lax.axis_index("samp")
    long = own.shape[1]

    def every(value):
        value = jnp.sum(value, 0)
        return value + pltpu.roll(value, STATS // 2, 0)

    for side, ref in enumerate((own, ahead)):
        pairs = ref[...].reshape(parts // 2, cols // long, STATS, long)
        for i in range(cols // long):
            stats = pairs[:, i]
            apart = (stats - every(stats)[None] / parts) + pltpu.roll(stats, STATS - 1, 1)
            apart = apart - every(apart)[None] / parts
            kind = lax.broadcasted_iota(jnp.int32, stats.shape, 1) % (STATS // 2)
            mark = jnp.where(kind == 0, apart, jnp.where(kind == 1, stats, 0.0))
            moved = every(mark * mark) * samples
            squares = every(stats)
            spread = (squares[2:3] + (moved[0:1] - moved[1:2])) / total
            here = slice(i * long, (i + 1) * long)
            marks[side * height : (side + 1) * height, here] = mark.reshape(height, long)
            place = 2 * height + side * STATS
            marks[place : place + STATS, here] = jnp.broadcast_to(lax.rsqrt(spread + EPS), (STATS, long))
    first = me * share
    if share % 128 == 0:
        rows = marks[:, pl.ds(pl.multiple_of(first, 128), share)]
    else:
        inside = lax.rem(first, 128)
        window = pl.ds(pl.multiple_of(first - inside, 128), 128)
        rows = pltpu.roll(marks[:, window], lax.rem(128 - inside, 128), 1)[:, :share]
    row_scale = rows[2 * height : 2 * height + 1] / total
    row_scale = jnp.broadcast_to(row_scale, (128, share)).T
    rows = rows[:height]
    kind = lax.broadcasted_iota(jnp.int32, rows.shape, 0) % (STATS // 2)
    signed = jnp.where(kind == 0, rows, jnp.where(kind == 1, -rows, 0.0)) * samples
    dot = functools.partial(
        lax.dot_general,
        dimension_numbers=(((0,), (0,)), ((), ())),
        precision=lax.Precision.HIGHEST,
        preferred_element_type=jnp.float32,
    )
    own_fix, ahead_fix = dot(signed, marks[:height, :]), dot(signed, marks[height : 2 * height, :])
    row = first + lax.broadcasted_iota(jnp.int32, (share, 128), 0)
    lane = lax.broadcasted_iota(jnp.int32, (share, 128), 1)
    for left in range(0, cols, 128):
        here = slice(left, left + 128)
        mine = lane + left > row
        own_scale = marks[2 * height : 2 * height + 1, here]
        ahead_scale = marks[2 * height + STATS : 2 * height + STATS + 1, here]
        fix[:, here] = jnp.where(mine, own_fix[:, here], ahead_fix[:, here])
        factor[:, here] = jnp.where(mine, own_scale, ahead_scale) * row_scale


def weigh(parts, samples, share, cols, own, ahead, after, weight):
    out = jax.ShapeDtypeStruct((share, cols), jnp.float32)
    return pl.pallas_call(
        functools.partial(weigh_kernel, parts, samples),
        in_specs=[VMEM, VMEM] + [ANY] * len(after),
        out_specs=[VMEM] * 2,
        out_shape=[out, out],
        scratch_shapes=[pltpu.VMEM(((parts + 2) * STATS, cols), jnp.float32)],
        compiler_params=params(16),
        cost_estimate=cost(weight),
        name="weigh",
    )(own, ahead, *after)


def finish_kernel(starts, sizes, fix, factor, *refs):
    out, body = refs[-2:]
    share, cols = out.shape
    first = lax.axis_index("samp") * share
    inside = lax.rem(first, 128)
    for i, start in enumerate(starts):
        mine = refs[sum(sizes[:i]) : sum(sizes[: i + 1])]
        for left in range(0, mine[0].shape[1], 128):
            total = sum(ref[:, left : left + 128] for ref in mine)
            here = slice(start + left, start + left + 128)
            there = lax.rem(start + left + cols - (first - inside), cols)
            there = pl.ds(pl.multiple_of(there, 128), 128)
            body[:, there] = (total + fix[:, here]) * factor[:, here]
    if share % 128:
        body[...] = pltpu.roll(body[...], lax.rem(cols - inside, cols), 1)
    tops = range(0, share, 8)
    turned = jnp.concatenate([pltpu.roll(body[top : top + 8, :], cols - top - 1, 1) for top in tops], 0)
    row = lax.broadcasted_iota(jnp.int32, (share, cols), 0)
    for step in (1, 2, 4):
        turned = jnp.where((row & step) != 0, pltpu.roll(turned, cols - step, 1), turned)
    out[...] = turned


def finish(starts, weights, sums):
    flat = [array for arrays in sums for array in arrays]
    sizes = [len(arrays) for arrays in sums]
    share, cols = weights[0].shape
    return pl.pallas_call(
        functools.partial(finish_kernel, starts, sizes),
        in_specs=[VMEM] * (2 + len(flat)),
        out_specs=VMEM,
        out_shape=jax.ShapeDtypeStruct((share, cols), jnp.float32),
        scratch_shapes=[pltpu.VMEM((share, cols), jnp.float32)],
        compiler_params=params(16),
        cost_estimate=cost(4),
        name="finish",
    )(*weights, *flat)


PLAN = (
    (0, 0, 0.01),
    (1, 0, 0.01),
    (0, 1, 3.2),
    (2, 0, 0.01),
    (0, 2, 0.01),
    (1, 1, 0.01),
    (3, 0, 0.01),
    (2, 1, 0.01),
    (1, 2, 0.01),
    (5, 0, 1.8),
    (4, 0, 0.01),
    (3, 1, 0.01),
    (1, 3, 0.6),
    (2, 2, 1.66),
    (4, 1, 2.5),
    (3, 2, 2.5),
    (4, 2, 0.01),
    (5, 1, 0.01),
    (2, 3, 1.6),
    (3, 3, 2.5),
)


def plan(steps, pieces):
    if steps == 3:
        return PLAN
    tasks = [(i, step, 1) for step in range(steps) for i in range(pieces)]
    return tasks + [(pieces, 0, 1), (pieces, 1, 1)]


def swap(array, bit, parts):
    return lax.ppermute(array, "samp", [(i, i ^ (1 << bit)) for i in range(parts)])


def local(dosages):
    samples, cols = dosages.shape
    parts = lax.axis_size("samp")
    blocks = lax.axis_size("var")
    share = cols // parts
    steps = parts.bit_length() - 1
    quarter, half = cols // 4, cols // 2
    route = [(i, i - 1) for i in range(1, blocks)]
    pieces = [
        (0, half, half, half),
        (0, cols, 0, quarter),
        (0, cols, quarter, quarter),
        (half, cols, half, quarter),
        (half, cols, half + quarter, quarter),
    ]
    prepared, stats, cuts = prepare(dosages, quarter, half)
    last = stats
    come = [[]] + [[lax.ppermute(cut, "var", route)] for cut in cuts]
    pairs, sums = {}, {}

    for i, step, weight in plan(steps, len(pieces)):
        after = [last]
        if i == len(pieces) and step == 0:
            stats = last = join(stats, after, weight)
            stats_next = lax.ppermute(stats, "var", route)
            continue
        if i == len(pieces):
            weights = weigh(parts, samples, share, cols, stats, stats_next, after, weight)
            last = weights[0]
            continue
        first, end, start, width = pieces[i]
        spots = parts * (end - first) // cols
        order = tuple(range(spots.bit_length() - 1))
        size = (end - first) >> step
        if step == 0:
            rows = [stats] if i == 0 else []
            send, last = gram(pieces[i], spots, order, prepared, come[i], rows, after, weight)
        elif step < steps - 1:
            rows = pairs[i][0].shape[0] - size
            send, last = add(size, pairs[i], 2, rows if step == 1 else 2 * rows, after, weight)
        elif step == steps:
            (last,) = sums[i] = add(share, pairs[i], 1, 0, after, weight)
            continue
        elif i == 0:
            pairs[i], stats = part(share, pairs[i], after, weight)
            last = pairs[i]
            stats = (stats, swap(stats, step, parts))
            continue
        elif end - first == cols:
            send, last = add(size, pairs[i], 2, 0, after, weight)
        else:
            send, last = cross(parts, start - half, pairs[i], pairs[0], after, weight)
        pairs[i] = (last, swap(send, step, parts))
    kept = range(1, len(pieces))
    return finish([pieces[i][2] for i in kept], weights, [sums.get(i, pairs[i]) for i in kept])


def solution(mesh):
    in_specs = (P("samp", "var"),)
    out_specs = P(("var", "samp"), None)
    return jax.shard_map(local, mesh=mesh, in_specs=in_specs, out_specs=out_specs, check_vma=False)
```

```python
import functools

import jax
import jax.numpy as jnp
from jax import lax
from jax.experimental import pallas as pl
from jax.experimental.pallas import tpu as pltpu
from jax.sharding import PartitionSpec as P

EPS = 1e-06
STATS = 8
VMEM = pl.BlockSpec(memory_space=pltpu.VMEM)
ANY = pl.BlockSpec(memory_space=pl.ANY)


def params(mib):
    return pltpu.CompilerParams(vmem_limit_bytes=mib << 20)


def cost(weight):
    return pl.CostEstimate(flops=int(weight * 1e9), bytes_accessed=1, transcendentals=0)


def split(value):
    high = value.astype(jnp.bfloat16)
    low = (value - high.astype(jnp.float32)).astype(jnp.bfloat16)
    return high, low


def centre(block):
    count = block.shape[0]
    mean = jnp.sum(block, 0, keepdims=True) / count
    centred = block - mean
    left = jnp.sum(centred, 0, keepdims=True) / count
    squares = jnp.sum(centred * centred, 0, keepdims=True)
    return centred, mean, left, squares


def prepare_kernel(dosages, high_t, low_t, stats, *refs):
    blocks, done = refs[:-1], refs[-1]
    width = blocks[0].shape[1]
    long = stats.shape[1]
    copies = []
    for i, block in enumerate(blocks):
        taken = dosages.at[:, pl.ds(i * width, width)]
        copies.append(pltpu.make_async_copy(taken, block, done.at[i]))
    for copy in copies:
        copy.start()
    for i, block in enumerate(blocks):
        copies[i].wait()
        here = pl.ds(i * width, width)
        centred, mean, left, squares = centre(block[...])
        high_t[here, :], low_t[here, :] = split(centred.T)
        rows = [mean, left, squares] + [jnp.zeros_like(mean)] * (STATS - 3)
        first = i * width // long * STATS
        stats[first : first + STATS, i * width % long : i * width % long + width] = jnp.concatenate(rows, 0)


def prepare(dosages, width, long):
    samples, cols = dosages.shape
    count = cols // width
    half_t = jax.ShapeDtypeStruct((cols, samples), jnp.bfloat16)
    stats = jax.ShapeDtypeStruct((STATS * cols // long, long), jnp.float32)
    block = jax.ShapeDtypeStruct((samples, width), jnp.float32)
    out = pl.pallas_call(
        prepare_kernel,
        in_specs=[pl.BlockSpec(memory_space=pltpu.HBM)],
        out_specs=[VMEM] * (3 + count),
        out_shape=[half_t, half_t, stats] + [block] * count,
        scratch_shapes=[pltpu.SemaphoreType.DMA((count,))],
        compiler_params=params(45),
        cost_estimate=cost(4),
        name="prepare",
    )(dosages)
    return out[:2], out[2], out[3:]


def place(owner, me, order):
    apart = jnp.bitwise_xor(owner, me)
    spot = 0
    for bit in order:
        spot = spot * 2 + (lax.shift_right_logical(apart, bit) & 1)
    return spot


def product(high_t, low_t, rows, high, low, side):
    sides = (((1,), (side,)), ((), ()))
    dot = functools.partial(lax.dot_general, dimension_numbers=sides, preferred_element_type=jnp.float32)
    a, b = high_t[rows, :], low_t[rows, :]
    return dot(a, high) + (dot(a, low) + dot(b, high))


def gram_kernel(piece, spots, order, ahead, rows, high_t, low_t, *refs):
    first, last, start, width = piece
    send, keep = refs[-2:]
    cols = high_t.shape[0]
    share = (last - first) // spots
    half = spots // 2
    me = lax.axis_index("samp")
    here = pl.ds(start, width)
    own_high, own_low = high_t[here, :], low_t[here, :]
    if rows:
        for out in (send, keep):
            out[half * share :, :] = refs[ahead][...]
    if ahead:
        ahead_high, ahead_low = split(centre(refs[0][...])[0])
    tall = min(width, 2 * cols // 8)
    for top in range(first, last, tall):
        band = pl.ds(top, tall)
        if top < start + width:
            tile = product(high_t, low_t, band, own_high, own_low, 1)
        if top + tall > start:
            later = product(high_t, low_t, band, ahead_high, ahead_low, 0)
            if top >= start + width:
                tile = later
            else:
                row = lax.broadcasted_iota(jnp.int32, tile.shape, 0) + top
                col = lax.broadcasted_iota(jnp.int32, tile.shape, 1) + start
                tile = jnp.where(col > row, tile, later)
        for part in range(tall // share):
            spot = place(top // share + part, me, order)
            block = tile[part * share : (part + 1) * share]
            there = pl.ds(pl.multiple_of((spot & (half - 1)) * share, share), share)

            @pl.when(spot >= half)
            def _():
                send[there, :] = block

            @pl.when(spot < half)
            def _():
                keep[there, :] = block


def gram(piece, spots, order, prepared, ahead, rows, after, weight):
    first, last, start, width = piece
    extra = sum(array.shape[0] for array in rows)
    out = jax.ShapeDtypeStruct(((last - first) // 2 + extra, width), jnp.float32)
    return pl.pallas_call(
        functools.partial(gram_kernel, piece, spots, order, len(ahead), extra),
        in_specs=[VMEM] * (2 + len(ahead) + len(rows)) + [ANY] * len(after),
        out_specs=[VMEM] * 2,
        out_shape=[out, out],
        compiler_params=params(24),
        cost_estimate=cost(weight),
        name="gram",
    )(*prepared, *ahead, *rows, *after)


def add_kernel(size, parts, extra, keep, got, *refs):
    out = refs[len(refs) - parts :]
    kept = size // parts
    rows = keep.shape[0] - size
    for i, ref in enumerate(out):
        here = slice((parts - 1 - i) * kept, (parts - i) * kept)
        ref[:kept, :] = keep[here, :] + got[here, :]
        if extra == rows and rows:
            far = got[size:, :].reshape(rows // STATS, STATS, -1)
            ref[kept:, :] = keep[size:, :] + pltpu.roll(far, STATS // 2, 1).reshape(rows, -1)
        elif rows:
            ref[kept : kept + rows, :] = keep[size:, :]
            ref[kept + rows :, :] = got[size:, :]


def add(size, pair, parts, extra, after, weight):
    cols = pair[0].shape[1]
    out = jax.ShapeDtypeStruct((size // parts + extra, cols), jnp.float32)
    return pl.pallas_call(
        functools.partial(add_kernel, size, parts, extra),
        in_specs=[VMEM, VMEM] + [ANY] * len(after),
        out_specs=[VMEM] * parts,
        out_shape=[out] * parts,
        compiler_params=params(16),
        cost_estimate=cost(weight),
        name="add",
    )(*pair, *after)


def part_kernel(size, keep, got, *refs):
    body, rows = refs[-2:]
    extra = keep.shape[0] - size
    body[...] = keep[:size, :] + got[:size, :]
    rows[:extra, :] = keep[size:, :]
    rows[extra:, :] = got[size:, :]


def part(size, pair, after, weight):
    rows, cols = pair[0].shape
    shapes = [(size, cols), (2 * (rows - size), cols)]
    return pl.pallas_call(
        functools.partial(part_kernel, size),
        in_specs=[VMEM, VMEM] + [ANY] * len(after),
        out_specs=[VMEM] * 2,
        out_shape=[jax.ShapeDtypeStruct(shape, jnp.float32) for shape in shapes],
        compiler_params=params(16),
        cost_estimate=cost(weight),
        name="part",
    )(*pair, *after)


def join_kernel(one, other, *refs):
    rows = one.shape[0]
    refs[-1][:rows, :] = one[...]
    refs[-1][rows:, :] = other[...]


def join(pair, after, weight):
    rows, cols = pair[0].shape
    return pl.pallas_call(
        join_kernel,
        in_specs=[VMEM, VMEM] + [ANY] * len(after),
        out_specs=VMEM,
        out_shape=jax.ShapeDtypeStruct((2 * rows, cols), jnp.float32),
        compiler_params=params(16),
        cost_estimate=cost(weight),
        name="join",
    )(*pair, *after)


def cross_kernel(parts, start, keep, got, early, *refs):
    send, mine = refs[-2:]
    total = keep[...] + got[...]
    other = early[:, start : start + total.shape[1]]
    upper = lax.axis_index("samp") >= parts // 2

    @pl.when(upper)
    def _():
        send[...] = other
        mine[...] = total

    @pl.when(jnp.logical_not(upper))
    def _():
        send[...] = total
        mine[...] = other


def cross(parts, start, pair, early, after, weight):
    out = jax.ShapeDtypeStruct(pair[0].shape, jnp.float32)
    return pl.pallas_call(
        functools.partial(cross_kernel, parts, start),
        in_specs=[VMEM] * 3 + [ANY] * len(after),
        out_specs=[VMEM] * 2,
        out_shape=[out, out],
        compiler_params=params(16),
        cost_estimate=cost(weight),
        name="cross",
    )(*pair, early, *after)


def weigh_kernel(parts, samples, own, ahead, *refs):
    fix, factor, marks = refs[-3:]
    share, cols = fix.shape
    total = samples * parts
    height = parts * STATS // 2
    me = lax.axis_index("samp")
    long = own.shape[1]

    def every(value):
        value = jnp.sum(value, 0)
        return value + pltpu.roll(value, STATS // 2, 0)

    for side, ref in enumerate((own, ahead)):
        pairs = ref[...].reshape(parts // 2, cols // long, STATS, long)
        for i in range(cols // long):
            stats = pairs[:, i]
            apart = (stats - every(stats)[None] / parts) + pltpu.roll(stats, STATS - 1, 1)
            apart = apart - every(apart)[None] / parts
            kind = lax.broadcasted_iota(jnp.int32, stats.shape, 1) % (STATS // 2)
            mark = jnp.where(kind == 0, apart, jnp.where(kind == 1, stats, 0.0))
            moved = every(mark * mark) * samples
            squares = every(stats)
            spread = (squares[2:3] + (moved[0:1] - moved[1:2])) / total
            here = slice(i * long, (i + 1) * long)
            marks[side * height : (side + 1) * height, here] = mark.reshape(height, long)
            place = 2 * height + side * STATS
            marks[place : place + STATS, here] = jnp.broadcast_to(lax.rsqrt(spread + EPS), (STATS, long))
    first = me * share
    if share % 128 == 0:
        rows = marks[:, pl.ds(pl.multiple_of(first, 128), share)]
    else:
        inside = lax.rem(first, 128)
        window = pl.ds(pl.multiple_of(first - inside, 128), 128)
        rows = pltpu.roll(marks[:, window], lax.rem(128 - inside, 128), 1)[:, :share]
    row_scale = rows[2 * height : 2 * height + 1] / total
    row_scale = jnp.broadcast_to(row_scale, (128, share)).T
    rows = rows[:height]
    kind = lax.broadcasted_iota(jnp.int32, rows.shape, 0) % (STATS // 2)
    signed = jnp.where(kind == 0, rows, jnp.where(kind == 1, -rows, 0.0)) * samples
    dot = functools.partial(
        lax.dot_general,
        dimension_numbers=(((0,), (0,)), ((), ())),
        precision=lax.Precision.HIGHEST,
        preferred_element_type=jnp.float32,
    )
    own_fix, ahead_fix = dot(signed, marks[:height, :]), dot(signed, marks[height : 2 * height, :])
    row = first + lax.broadcasted_iota(jnp.int32, (share, 128), 0)
    lane = lax.broadcasted_iota(jnp.int32, (share, 128), 1)
    for left in range(0, cols, 128):
        here = slice(left, left + 128)
        mine = lane + left > row
        own_scale = marks[2 * height : 2 * height + 1, here]
        ahead_scale = marks[2 * height + STATS : 2 * height + STATS + 1, here]
        fix[:, here] = jnp.where(mine, own_fix[:, here], ahead_fix[:, here])
        factor[:, here] = jnp.where(mine, own_scale, ahead_scale) * row_scale


def weigh(parts, samples, share, cols, own, ahead, after, weight):
    out = jax.ShapeDtypeStruct((share, cols), jnp.float32)
    return pl.pallas_call(
        functools.partial(weigh_kernel, parts, samples),
        in_specs=[VMEM, VMEM] + [ANY] * len(after),
        out_specs=[VMEM] * 2,
        out_shape=[out, out],
        scratch_shapes=[pltpu.VMEM(((parts + 2) * STATS, cols), jnp.float32)],
        compiler_params=params(16),
        cost_estimate=cost(weight),
        name="weigh",
    )(own, ahead, *after)


def finish_kernel(starts, sizes, fix, factor, *refs):
    out, body = refs[-2:]
    share, cols = out.shape
    first = lax.axis_index("samp") * share
    inside = lax.rem(first, 128)
    for i, start in enumerate(starts):
        mine = refs[sum(sizes[:i]) : sum(sizes[: i + 1])]
        for left in range(0, mine[0].shape[1], 128):
            total = sum(ref[:, left : left + 128] for ref in mine)
            here = slice(start + left, start + left + 128)
            there = lax.rem(start + left + cols - (first - inside), cols)
            there = pl.ds(pl.multiple_of(there, 128), 128)
            body[:, there] = (total + fix[:, here]) * factor[:, here]
    if share % 128:
        body[...] = pltpu.roll(body[...], lax.rem(cols - inside, cols), 1)
    tops = range(0, share, 8)
    turned = jnp.concatenate([pltpu.roll(body[top : top + 8, :], cols - top - 1, 1) for top in tops], 0)
    row = lax.broadcasted_iota(jnp.int32, (share, cols), 0)
    for step in (1, 2, 4):
        turned = jnp.where((row & step) != 0, pltpu.roll(turned, cols - step, 1), turned)
    out[...] = turned


def finish(starts, weights, sums):
    flat = [array for arrays in sums for array in arrays]
    sizes = [len(arrays) for arrays in sums]
    share, cols = weights[0].shape
    return pl.pallas_call(
        functools.partial(finish_kernel, starts, sizes),
        in_specs=[VMEM] * (2 + len(flat)),
        out_specs=VMEM,
        out_shape=jax.ShapeDtypeStruct((share, cols), jnp.float32),
        scratch_shapes=[pltpu.VMEM((share, cols), jnp.float32)],
        compiler_params=params(16),
        cost_estimate=cost(4),
        name="finish",
    )(*weights, *flat)


PLAN = (
    (0, 0, 0.01),
    (1, 0, 0.01),
    (0, 1, 3.2),
    (2, 0, 0.01),
    (0, 2, 0.01),
    (1, 1, 0.01),
    (3, 0, 0.01),
    (2, 1, 0.01),
    (1, 2, 0.01),
    (5, 0, 1.8),
    (4, 0, 0.01),
    (3, 1, 0.01),
    (1, 3, 0.6),
    (2, 2, 1.66),
    (4, 1, 2.5),
    (3, 2, 2.5),
    (4, 2, 0.01),
    (2, 3, 1.6),
    (3, 3, 2.5),
    (5, 1, 0.01),
)


def plan(steps, pieces):
    if steps == 3:
        return PLAN
    tasks = [(i, step, 1) for step in range(steps) for i in range(pieces)]
    return tasks + [(pieces, 0, 1), (pieces, 1, 1)]


def swap(array, bit, parts):
    return lax.ppermute(array, "samp", [(i, i ^ (1 << bit)) for i in range(parts)])


def local(dosages):
    samples, cols = dosages.shape
    parts = lax.axis_size("samp")
    blocks = lax.axis_size("var")
    share = cols // parts
    steps = parts.bit_length() - 1
    quarter, half = cols // 4, cols // 2
    route = [(i, i - 1) for i in range(1, blocks)]
    pieces = [
        (0, half, half, half),
        (0, cols, 0, quarter),
        (0, cols, quarter, quarter),
        (half, cols, half, quarter),
        (half, cols, half + quarter, quarter),
    ]
    prepared, stats, cuts = prepare(dosages, quarter, half)
    last = stats
    come = [[]] + [[lax.ppermute(cut, "var", route)] for cut in cuts]
    pairs, sums = {}, {}

    for i, step, weight in plan(steps, len(pieces)):
        after = [last]
        if i == len(pieces) and step == 0:
            stats = last = join(stats, after, weight)
            stats_next = lax.ppermute(stats, "var", route)
            continue
        if i == len(pieces):
            weights = weigh(parts, samples, share, cols, stats, stats_next, after, weight)
            last = weights[0]
            continue
        first, end, start, width = pieces[i]
        spots = parts * (end - first) // cols
        order = tuple(range(spots.bit_length() - 1))
        size = (end - first) >> step
        if step == 0:
            rows = [stats] if i == 0 else []
            send, last = gram(pieces[i], spots, order, prepared, come[i], rows, after, weight)
        elif step < steps - 1:
            rows = pairs[i][0].shape[0] - size
            send, last = add(size, pairs[i], 2, rows if step == 1 else 2 * rows, after, weight)
        elif step == steps:
            (last,) = sums[i] = add(share, pairs[i], 1, 0, after, weight)
            continue
        elif i == 0:
            pairs[i], stats = part(share, pairs[i], after, weight)
            last = pairs[i]
            stats = (stats, swap(stats, step, parts))
            continue
        elif end - first == cols:
            send, last = add(size, pairs[i], 2, 0, after, weight)
        else:
            send, last = cross(parts, start - half, pairs[i], pairs[0], after, weight)
        pairs[i] = (last, swap(send, step, parts))
    kept = range(1, len(pieces))
    return finish([pieces[i][2] for i in kept], weights, [sums.get(i, pairs[i]) for i in kept])


def solution(mesh):
    in_specs = (P("samp", "var"),)
    out_specs = P(("var", "samp"), None)
    return jax.shard_map(local, mesh=mesh, in_specs=in_specs, out_specs=out_specs, check_vma=False)
```
